32 devices in a mesh: dp: 8 (over z, core), seq: 4 (over y, x).
Axes of the slice: x: 2, y: 2, z: 4, core: 2. Of those that a mesh axis runs over, the one named last changes fastest.
Arguments:
- tokens_in: bfloat16 [8, 2048, 2048], P('dp', 'seq'), may hold values from -6 to 6
- grad_out: bfloat16 [8, 2048, 2048], P('dp', 'seq'), may hold values from -6 to 6
- seq_lengths: int32 [8], P('dp'), may hold values from 512 to 2048, as said below
- stretch_order: int32 [8, 8], P('dp'), may hold values from 0 to 7, each once within a row
- attn_gain: bfloat16 [2048], P(('dp', 'seq')), may hold values from 0.5 to 1.5
- query_w: bfloat16 [2048, 2048], P(('dp', 'seq')), may hold values from -0.125 to 0.125
- key_w: bfloat16 [2048, 512], P(('dp', 'seq')), may hold values from -0.125 to 0.125
- value_w: bfloat16 [2048, 512], P(('dp', 'seq')), may hold values from -0.125 to 0.125
- output_w: bfloat16 [2048, 2048], P(('dp', 'seq')), may hold values from -0.75 to 0.75
- mlp_gain: bfloat16 [2048], P(('dp', 'seq')), may hold values from 0.5 to 1.5
- gate_w: bfloat16 [2048, 8192], P(('dp', 'seq')), may hold values from -0.125 to 0.125
- up_w: bfloat16 [2048, 8192], P(('dp', 'seq')), may hold values from -0.125 to 0.125
- down_w: bfloat16 [2048, 8192], P(('dp', 'seq')), may hold values from -0.0625 to 0.0625
Outputs:
- tokens_out: bfloat16 [8, 2048, 2048], P('dp', 'seq')
- tokens_grad: float32 [8, 2048, 2048], P('dp', 'seq')
- attn_gain_grad: float32 [2048], P(('dp', 'seq'))
- query_grad: float32 [2048, 2048], P(('dp', 'seq'))
- key_grad: float32 [2048, 512], P(('dp', 'seq'))
- value_grad: float32 [2048, 512], P(('dp', 'seq'))
- output_grad: float32 [2048, 2048], P(('dp', 'seq'))
- mlp_gain_grad: float32 [2048], P(('dp', 'seq'))
- gate_grad: float32 [2048, 8192], P(('dp', 'seq'))
- up_grad: float32 [2048, 8192], P(('dp', 'seq'))
- down_grad: float32 [2048, 8192], P(('dp', 'seq'))
The draws below stay inside these ranges and needn't reach their ends.
Inputs may be any that keep to these rules, and one draw needn't show every extreme that they name: `seq_lengths`: in every draw some sequence is full. Each row is a permutation; stored block c of sequence s holds positions stretch_order[s, c] * 256 to stretch_order[s, c] * 256 + 255.
All inputs are finite; a program needn't handle non-finite values.
Results may differ from the reference program's by a relative error of at most 0.017.
Values may be sent and summed in bfloat16 or wider, within the bound.
A program may use at most 704 MiB of HBM per device.

```python
import math
import jax
import jax.numpy as jnp
from jax import lax

D = 2048
HEADS = 32
KVH = 8
HD = 64
FF = 8192
LEN = 2048
SEQS = 8
NCH = 8
CH = 256


def draw_seq_lengths(key, part):
    span = 3 * LEN // 4 + 1
    first_draw = jax.random.randint(jax.random.fold_in(key, 11), (SEQS,), 0, span)
    second_draw = jax.random.randint(jax.random.fold_in(key, 12), (SEQS,), 0, span)
    third_draw = jax.random.randint(jax.random.fold_in(key, 13), (SEQS,), 0, span)
    shortfall = jnp.minimum(jnp.minimum(first_draw, second_draw), third_draw)
    full_index = jax.random.randint(jax.random.fold_in(key, 14), (), 0, SEQS)
    shortfall = jnp.where(jnp.arange(SEQS) == full_index, 0, shortfall)
    return (LEN - shortfall).astype(jnp.int32)


def levels(key, extent, cuts, low, high):
    def one(dim, shards_of):
        steps = jax.random.uniform(jax.random.fold_in(jax.random.fold_in(key, 6), dim), (shards_of,), jnp.float32, low / len(cuts), high / len(cuts))
        return jnp.repeat(jnp.exp(steps), extent[dim] // shards_of).reshape((-1,) + (1,) * (len(extent) - dim - 1))

    gain = one(*cuts[0])
    for cut in cuts[1:]:
        gain = gain * one(*cut)
    return gain


def gaussian(rng, dims, scale, reach, shards=(), held_as=jnp.bfloat16):
    gain = levels(rng, dims, shards, -0.22, 0.18) if shards else 1.0
    drawn = jax.random.normal(rng, dims, jnp.float32) * scale * gain
    return jnp.minimum(jnp.maximum(drawn, -reach), reach).astype(held_as)


def setup_inputs(seed: int = 0) -> dict:
    seeds = jax.random.split(jax.random.key(seed), 14)
    tokens_in = gaussian(seeds[0], (SEQS, LEN, D), 1.0, 6.0, ((0, 8), (1, 4)))
    grad_out = gaussian(seeds[1], (SEQS, LEN, D), 1.0, 6.0, ((0, 8), (1, 4)))
    seq_lengths = draw_seq_lengths(jax.random.fold_in(seeds[13], 71), 0)
    stretch_order = jax.vmap(lambda own: jax.random.permutation(own, NCH))(jax.random.split(seeds[3], SEQS)).reshape((SEQS, NCH)).astype(jnp.int32)
    attn_gain = jnp.clip(1.0 + 0.1 * jax.random.normal(seeds[4], (D,), jnp.float32), 0.5, 1.5).astype(jnp.bfloat16)
    query_w = gaussian(seeds[5], (D, D), D ** -0.5, 0.125, ((0, 32),))
    key_w = gaussian(seeds[6], (D, KVH * HD), D ** -0.5, 0.125, ((0, 32),))
    value_w = gaussian(seeds[7], (D, KVH * HD), D ** -0.5, 0.125, ((0, 32),))
    output_w = gaussian(seeds[8], (D, D), (D // 32) ** -0.5, 0.75, ((0, 32),))
    mlp_gain = jnp.clip(1.0 + 0.1 * jax.random.normal(seeds[9], (D,), jnp.float32), 0.5, 1.5).astype(jnp.bfloat16)
    gate_w = gaussian(seeds[10], (D, FF), D ** -0.5, 0.125, ((0, 32),))
    up_w = gaussian(seeds[11], (D, FF), D ** -0.5, 0.125, ((0, 32),))
    down_w = gaussian(seeds[12], (D, FF), FF ** -0.5, 0.0625, ((0, 32),))
    return dict(tokens_in=tokens_in, grad_out=grad_out, seq_lengths=seq_lengths, stretch_order=stretch_order, attn_gain=attn_gain, query_w=query_w, key_w=key_w, value_w=value_w, output_w=output_w, mlp_gain=mlp_gain, gate_w=gate_w, up_w=up_w, down_w=down_w)


epsilon = 1e-05
masked_score = -1e+30
highest = lax.Precision.HIGHEST

@jax.custom_vjp
def low(v):
    return lax.optimization_barrier(v.astype(jnp.bfloat16)).astype(jnp.float32)

@jax.custom_vjp
def low_back(v):
    return v

def low_keep(v):
    return (low(v), None)

def low_pass(kept, grad):
    return (grad,)

def back_keep(v):
    return (v, None)

def back_low(kept, grad):
    return (low(grad),)
low.defvjp(low_keep, low_pass)
low_back.defvjp(back_keep, back_low)

def frequencies():
    steps_even = jnp.arange(0, HD, 2).astype(jnp.float32) / HD
    base_freq = 1.0 / 500000.0 ** steps_even
    wavelength = 2.0 * math.pi / base_freq
    smooth = (8192.0 / wavelength - 1.0) / 3.0
    blended = (1.0 - smooth) * base_freq / 32.0 + smooth * base_freq
    return jnp.where(wavelength < 2048.0, base_freq, jnp.where(wavelength > 8192.0, base_freq / 32.0, blended))

def rotate(vectors, cos_table, sin_table):
    middle_at = vectors.shape[-1] // 2
    first_half = vectors[..., :middle_at]
    second_half = vectors[..., middle_at:]
    return jnp.concatenate([first_half * cos_table - second_half * sin_table, second_half * cos_table + first_half * sin_table], axis=-1)

def matmul_full(left_side, right_side):
    return jnp.dot(left_side, right_side, precision=highest, preferred_element_type=jnp.float32)

def layer(inputs, attn_gain, query_w, key_w, value_w, output_w, mlp_gain, gate_w, up_w, down_w, positions, seq_length):
    repeat = HEADS // KVH
    angles = positions.astype(jnp.float32)[:, None] * frequencies()[None, :]
    cos_table = jnp.cos(angles)[:, None, :]
    sin_table = jnp.sin(angles)[:, None, :]
    scale_one = lax.rsqrt(lax.optimization_barrier(jnp.mean(inputs * inputs, axis=1, keepdims=True)) + epsilon)
    normed_one = low(inputs * scale_one * attn_gain)
    queries = low_back(matmul_full(normed_one, query_w)).reshape(LEN, HEADS, HD)
    key_pre = low_back(matmul_full(normed_one, key_w)).reshape(LEN, KVH, HD)
    value_rows = low_back(low(matmul_full(normed_one, value_w))).reshape(LEN, KVH, HD)
    query_rot = low(rotate(queries, cos_table, sin_table)).reshape(LEN, KVH, repeat, HD)
    key_rot = low(rotate(key_pre, cos_table, sin_table))
    key_live = positions < seq_length
    block_rows = min(LEN, 512)

    def attend_block(block_pair):
        query_block, pos_block = block_pair
        scores = low_back(jnp.einsum('qgrd,kgd->grqk', query_block, key_rot, precision=highest) * 0.125)
        allowed = (positions[None, :] <= pos_block[:, None]) & key_live[None, :]
        scores = jnp.where(allowed[None, None], scores, masked_score)
        probs = low(jax.nn.softmax(scores, axis=-1))
        return jnp.einsum('grqk,kgd->qgrd', probs, value_rows, precision=highest)
    attended = lax.map(jax.checkpoint(attend_block), (query_rot.reshape(LEN // block_rows, block_rows, KVH, repeat, HD), positions.reshape(LEN // block_rows, block_rows)))
    attended = low_back(low(attended.reshape(LEN, HEADS * HD)))
    middle = inputs + low_back(jnp.dot(attended, output_w.T, precision=highest, preferred_element_type=jnp.float32))
    scale_two = lax.rsqrt(lax.optimization_barrier(jnp.mean(middle * middle, axis=1, keepdims=True)) + epsilon)
    normed_two = low(middle * scale_two * mlp_gain)
    gate_pre = low_back(matmul_full(normed_two, gate_w))
    up_pre = low_back(matmul_full(normed_two, up_w))
    hidden = low(jax.nn.silu(gate_pre) * up_pre)
    branch_two = low_back(jnp.dot(hidden, down_w.T, precision=highest, preferred_element_type=jnp.float32))
    return (middle + branch_two) * key_live.astype(jnp.float32)[:, None]

def reference(tokens_in, grad_out, seq_lengths, stretch_order, attn_gain, query_w, key_w, value_w, output_w, mlp_gain, gate_w, up_w, down_w):
    params = tuple((weight.astype(jnp.float32) for weight in (attn_gain, query_w, key_w, value_w, output_w, mlp_gain, gate_w, up_w, down_w)))
    offsets = jnp.arange(CH, dtype=jnp.int32)

    def one_sequence(summed, item_set):
        tokens, grads, seq_length, order_row = item_set
        positions = (order_row.astype(jnp.int32)[:, None] * CH + offsets[None, :]).reshape(LEN).astype(jnp.int32)

        def forward(inputs, *weights):
            return layer(inputs, *weights, positions, seq_length)
        result, pull = jax.vjp(forward, tokens.astype(jnp.float32), *params)
        pulled = pull(grads.astype(jnp.float32))
        summed = tuple((total_now + gradient for total_now, gradient in zip(summed, pulled[1:])))
        return (summed, (result.astype(jnp.bfloat16), pulled[0]))
    start = tuple((jnp.zeros(param.shape, jnp.float32) for param in params))
    totals, (results, input_grads) = lax.scan(one_sequence, start, (tokens_in, grad_out, seq_lengths, stretch_order))
    return (results, input_grads, totals[0], totals[1], totals[2], totals[3], totals[4], totals[5], totals[6], totals[7], totals[8])
```

```python
import functools
import math

import jax
import jax.numpy as jnp
from jax import lax
from jax.experimental import pallas as pl
from jax.experimental.pallas import tpu as pltpu
from jax.sharding import Mesh
from jax.sharding import PartitionSpec as P

HEADS = 32
KVH = 8
HD = 64
REP = HEADS // KVH

epsilon = 1e-05
masked_score = -1e30
floor_score = -1e29

bf16 = jnp.bfloat16
f32 = jnp.float32


def frequencies():
    steps_even = jnp.arange(0, HD, 2).astype(f32) / HD
    base_freq = 1.0 / 500000.0**steps_even
    wavelength = 2.0 * math.pi / base_freq
    smooth = (8192.0 / wavelength - 1.0) / 3.0
    blended = (1.0 - smooth) * base_freq / 32.0 + smooth * base_freq
    return jnp.where(
        wavelength < 2048.0, base_freq, jnp.where(wavelength > 8192.0, base_freq / 32.0, blended)
    )


def shift(value, axis, steps):
    size = lax.axis_size(axis)
    return lax.ppermute(value, axis, [(i, (i + steps) % size) for i in range(size)])


def in_order(own, other, index, axis):
    return jnp.where(
        index == 0,
        jnp.concatenate([own, other], axis=axis),
        jnp.concatenate([other, own], axis=axis),
    )


def halves(value, index, axis):
    size = value.shape[axis] // 2
    return (
        lax.dynamic_slice_in_dim(value, index * size, size, axis),
        lax.dynamic_slice_in_dim(value, (1 - index) * size, size, axis),
    )


def spread_columns(shard, c, x, earlier=(), later=()):
    own, other = halves(shard, x, 1)
    if earlier:
        other = hold(other, *earlier)
    both = in_order(own, after(shift(other, "x", 1), *later), x, 0)
    own, other = halves(both, c, 1)
    return in_order(own, shift(other, "c", 1), c, 0)


def join_columns(unit, c, x):
    own, other = halves(unit, c, 0)
    both = in_order(own, shift(other, "c", 1), c, 1)
    own, other = halves(both, x, 0)
    return in_order(own, shift(other, "x", 1), x, 1)


def after(value, *others):
    return lax.optimization_barrier((value,) + others)[0]


def hold_body(*refs):
    del refs


def hold(value, *others):
    return pl.pallas_call(
        hold_body,
        in_specs=[pl.BlockSpec(memory_space=pl.ANY)] * (1 + len(others)),
        out_specs=pl.BlockSpec(memory_space=pl.ANY),
        out_shape=jax.ShapeDtypeStruct(value.shape, value.dtype),
        input_output_aliases={0: 0},
        name="hold",
    )(value, *others)


def gather_column(unit):
    return lax.all_gather(unit, "z", axis=0, tiled=True)


def gather_slots(column):
    return [column] + [shift(column, "y", k) for k in range(1, lax.axis_size("y"))]


def send_slots(terms):
    return [shift(term, "y", -(k + 1)) for k, term in enumerate(terms)]


def gather_whole(unit, y):
    zs, ys = lax.axis_size("z"), lax.axis_size("y")
    size = zs * unit.shape[0]
    whole = lax.all_gather(unit, ("y", "z"), axis=0, tiled=True)
    return [lax.dynamic_slice_in_dim(whole, ((y - k) % ys) * size, size, 0) for k in range(ys)]


def scatter_whole(terms):
    return lax.psum_scatter(terms, ("y", "z"), scatter_dimension=0, tiled=True)


def scatter_column(total):
    return lax.psum_scatter(total, "z", scatter_dimension=0, tiled=True)


def gather_gains(unit):
    zs, ys = lax.axis_size("z"), lax.axis_size("y")
    row = jnp.stack([unit] + [shift(unit, "y", k) for k in range(1, ys)], axis=1)
    z = lax.axis_index("z")
    out = jnp.zeros((2, ys, zs, unit.shape[1]), unit.dtype)
    for j in range(zs):
        got = row if j == 0 else shift(row, "z", j)
        out = lax.dynamic_update_slice(out, got[:, :, None], (0, 0, (z - j) % zs, 0))
    return out.reshape(2, -1)


def scatter_gains(terms, unit):
    zs, ys = lax.axis_size("z"), lax.axis_size("y")
    z = lax.axis_index("z")
    terms = terms.reshape(ys, zs * unit)
    total = terms[0]
    for k in range(1, ys):
        total = total + shift(terms[k], "y", -k)
    total = total.reshape(zs, unit)
    out = lax.dynamic_index_in_dim(total, z, 0, keepdims=False)
    for j in range(1, zs):
        out = out + shift(lax.dynamic_index_in_dim(total, (z - j) % zs, 0, keepdims=False), "z", -j)
    return out


def gather_tokens(own, *others):
    beside = after(shift(own, "x", 1), *others)
    sibling = shift(own, "c", 1)
    return jnp.concatenate([own, beside, sibling, shift(beside, "c", 1)], axis=0)


def scatter_tokens(partials):
    sums = []
    for partial in partials:
        count = partial.shape[0] // 4
        half = partial[: 2 * count].astype(f32) + shift(partial[2 * count :], "c", 1).astype(f32)
        sums.append(half[:count] + shift(half[count:].astype(bf16), "x", 1).astype(f32))
    return jnp.concatenate(sums, axis=1)


def move_columns_body(zs, ys, forth, y_ref, in_ref, out_ref):
    block = in_ref.shape[1] // (zs * 2 * ys)
    y = y_ref[0]
    for i in range(zs * 2):
        for k in range(ys):
            natural = i * ys + lax.rem(y - k + ys, ys)
            natural = pl.ds(pl.multiple_of(natural * block, block), block)
            slot = pl.ds((k * zs * 2 + i) * block, block)
            if forth:
                out_ref[:, slot] = in_ref[:, natural]
            else:
                out_ref[:, natural] = in_ref[:, slot]


def move_columns(value, y, zs, ys, forth):
    rows, width = value.shape
    tall = rows // 4
    spec = pl.BlockSpec((tall, width), lambda i, *_: (i, 0))
    return pl.pallas_call(
        functools.partial(move_columns_body, zs, ys, forth),
        grid_spec=pltpu.PrefetchScalarGridSpec(
            num_scalar_prefetch=1, grid=(4,), in_specs=[spec], out_specs=spec
        ),
        out_shape=jax.ShapeDtypeStruct(value.shape, value.dtype),
        cost_estimate=pl.CostEstimate(
            flops=0, bytes_accessed=2 * value.size * value.dtype.itemsize, transcendentals=0
        ),
        name="move_columns",
    )(y, value)


VMEM_BYTES = 56 * 1024 * 1024
EASE = 1


def estimate(flops, moved, exps=0):
    return pl.CostEstimate(
        flops=int(flops) // EASE, bytes_accessed=int(moved) // EASE, transcendentals=int(exps) // EASE
    )


def fit(size, most):
    return size if size <= most else fit(size // 2, most)


def rows_product(left, parts, extras, finish, n_out, name):
    t, d = left.shape
    n = parts[0].shape[1]
    depth = parts[0].shape[0]
    bm, bn = fit(t, 512), fit(n, 1024)
    n_parts, n_extra = len(parts), len(extras)

    def kernel(*refs):
        left_ref = refs[0]
        product = None
        for p in range(n_parts):
            term = jnp.dot(
                left_ref[:, p * depth : (p + 1) * depth], refs[1 + p][...], preferred_element_type=f32
            )
            product = term if product is None else product + term
        got = finish(product, *(r[...] for r in refs[1 + n_parts : 1 + n_parts + n_extra]))
        for ref, value in zip(refs[1 + n_parts + n_extra :], got):
            ref[...] = value.astype(bf16)

    tile = pl.BlockSpec((bm, bn), lambda j, i: (i, j))
    return pl.pallas_call(
        kernel,
        grid=(n // bn, t // bm),
        in_specs=[pl.BlockSpec((bm, d), lambda j, i: (i, 0))]
        + [pl.BlockSpec((depth, bn), lambda j, i: (0, j))] * n_parts
        + [tile] * n_extra,
        out_specs=[tile] * n_out,
        out_shape=[jax.ShapeDtypeStruct((t, n), bf16)] * n_out,
        compiler_params=pltpu.CompilerParams(vmem_limit_bytes=VMEM_BYTES),
        cost_estimate=estimate(2 * t * d * n, 2 * (t * d + d * n + t * n)),
        name=name,
    )(left, *parts, *extras)


def turned_product(lefts, rights, name):
    t, f = lefts[0].shape
    n = rights[0].shape[0]
    bm, bn = fit(t, 512), fit(n, 1024)
    count = len(lefts)

    def kernel(*refs):
        product = None
        for p in range(count):
            term = lax.dot_general(
                refs[p][...], refs[count + p][...], (((1,), (1,)), ((), ())), preferred_element_type=f32
            )
            product = term if product is None else product + term
        refs[2 * count][...] = product.astype(bf16)

    return pl.pallas_call(
        kernel,
        grid=(n // bn, t // bm),
        in_specs=[pl.BlockSpec((bm, f), lambda j, i: (i, 0))] * count
        + [pl.BlockSpec((bn, f), lambda j, i: (j, 0))] * count,
        out_specs=pl.BlockSpec((bm, bn), lambda j, i: (i, j)),
        out_shape=jax.ShapeDtypeStruct((t, n), bf16),
        compiler_params=pltpu.CompilerParams(vmem_limit_bytes=VMEM_BYTES),
        cost_estimate=estimate(2 * count * t * f * n, 2 * count * (t * f + f * n)),
        name=name,
    )(*lefts, *rights)


def columns_product(left, slots, n_parts, right, others, name):
    t, d = left.shape
    m = d // n_parts
    f = right.shape[1]
    bm, bn = fit(m, 512), fit(f, 1024)
    per = m // bm
    count = len(others)

    def kernel(slots_ref, left_ref, right_ref, *refs):
        turned_ref = refs[-1]

        @pl.when(pl.program_id(1) == 0)
        def _():
            turned_ref[...] = left_ref[...].T

        product = jnp.dot(turned_ref[...], right_ref[...], preferred_element_type=f32)
        for ref in refs[:count]:
            product = product + ref[...].astype(f32)
        refs[count][...] = product.astype(bf16)

    rows = slots.shape[0] * m
    tile = pl.BlockSpec((bm, bn), lambda i, j, slots_ref: (i, j))
    return pl.pallas_call(
        kernel,
        grid_spec=pltpu.PrefetchScalarGridSpec(
            num_scalar_prefetch=1,
            grid=(rows // bm, f // bn),
            in_specs=[
                pl.BlockSpec((t, bm), lambda i, j, slots_ref: (0, slots_ref[i // per] * per + i % per)),
                pl.BlockSpec((t, bn), lambda i, j, slots_ref: (0, j)),
            ]
            + [tile] * count,
            out_specs=tile,
            scratch_shapes=[pltpu.VMEM((bm, t), bf16)],
        ),
        out_shape=jax.ShapeDtypeStruct((rows, f), bf16),
        compiler_params=pltpu.CompilerParams(vmem_limit_bytes=VMEM_BYTES),
        cost_estimate=estimate(2 * t * rows * f, 2 * (t * m + t * f + rows * f)),
        name=name,
    )(slots, left, right, *others)


def plain(product):
    return (product,)


def up_finish(product, gate):
    gate = gate.astype(f32)
    return product, gate * jax.nn.sigmoid(gate) * product


def hidden_back(grad, gate, up):
    gate, up = gate.astype(f32), up.astype(f32)
    sigmoid = jax.nn.sigmoid(gate)
    return grad * up * sigmoid * (1.0 + gate * (1.0 - sigmoid)), grad * gate * sigmoid


def attention_fwd_body(
    chunk, blocks, qpos_ref, kpos_ref, len_ref, q_ref, k_ref, v_ref, o_ref, lse_ref,
    kn_ref, m_ref, l_ref, acc_ref,
):
    s, qb = pl.program_id(0), pl.program_id(2)
    ys = k_ref.shape[0]

    @pl.when(qb == 0)
    def _():
        for yk in range(ys):
            for b in range(blocks):
                kn_ref[pl.ds((yk * blocks + b) * chunk, chunk), :] = (
                    k_ref[yk, :, pl.ds(b * chunk, chunk)].astype(f32).T.astype(bf16)
                )

    qp = qpos_ref[s, qb]
    length = len_ref[s]
    m_ref[...] = jnp.full_like(m_ref, floor_score)
    l_ref[...] = jnp.zeros_like(l_ref)
    acc_ref[...] = jnp.zeros_like(acc_ref)

    for yk in range(ys):

        def step(b, carry, yk=yk):
            kp = kpos_ref[s, yk * blocks + b]
            first = kp * chunk
            live = (kp <= qp) & (first < length)
            partly = (kp == qp) | (first + chunk > length)

            def work(masked):
                kn = kn_ref[pl.ds(pl.multiple_of((yk * blocks + b) * chunk, chunk), chunk), :]
                vt = v_ref[yk, :, pl.ds(pl.multiple_of(b * chunk, chunk), chunk)]
                if masked:
                    at_key = first + lax.broadcasted_iota(jnp.int32, (chunk, chunk), 0)
                    at_query = qp * chunk + lax.broadcasted_iota(jnp.int32, (chunk, chunk), 1)
                    allowed = (at_key <= at_query) & (at_key < length)
                for h in range(REP):
                    rows = slice(h * HD, (h + 1) * HD)
                    scores = jnp.dot(kn, q_ref[rows, :], preferred_element_type=f32)
                    if masked:
                        scores = jnp.where(allowed, scores, masked_score)
                    m_old = m_ref[h : h + 1, :]
                    m_new = jnp.maximum(m_old, jnp.max(scores, axis=0, keepdims=True))
                    alpha = jnp.exp(m_old - m_new)
                    probs = jnp.exp(scores - m_new)
                    m_ref[h : h + 1, :] = m_new
                    l_ref[h : h + 1, :] = l_ref[h : h + 1, :] * alpha + jnp.sum(
                        probs, axis=0, keepdims=True
                    )
                    acc_ref[rows, :] = acc_ref[rows, :] * alpha + jnp.dot(
                        vt, probs.astype(bf16), preferred_element_type=f32
                    )

            pl.when(live & partly)(lambda: work(True))
            pl.when(live & jnp.logical_not(partly))(lambda: work(False))
            return carry

        lax.fori_loop(0, blocks, step, 0)

    for h in range(REP):
        rows = slice(h * HD, (h + 1) * HD)
        o_ref[rows, :] = (acc_ref[rows, :] / l_ref[h : h + 1, :]).astype(bf16)
    lse_ref[0] = m_ref[0:REP, :] + jnp.log(l_ref[0:REP, :])


def attention_fwd(queries, keys, values, qpos, kpos, lengths, chunk):
    tokens = queries.shape[1]
    groups = queries.shape[0] // (REP * HD)
    ys = keys.shape[0]
    half = tokens // 2
    blocks = half // chunk
    grid = (2, groups, blocks)
    q_spec = pl.BlockSpec((REP * HD, chunk), lambda s, g, b, *_: (g, s * blocks + b))
    kv_spec = pl.BlockSpec((ys, HD, half), lambda s, g, b, *_: (0, g, s))
    lse_spec = pl.BlockSpec((1, REP, chunk), lambda s, g, b, *_: (g, 0, s * blocks + b))
    pairs = 2 * groups * blocks * blocks * ys
    return pl.pallas_call(
        functools.partial(attention_fwd_body, chunk, blocks),
        grid_spec=pltpu.PrefetchScalarGridSpec(
            num_scalar_prefetch=3,
            grid=grid,
            in_specs=[q_spec, kv_spec, kv_spec],
            out_specs=[q_spec, lse_spec],
            scratch_shapes=[
                pltpu.VMEM((ys * half, HD), bf16),
                pltpu.VMEM((8, chunk), f32),
                pltpu.VMEM((8, chunk), f32),
                pltpu.VMEM((REP * HD, chunk), f32),
            ],
        ),
        out_shape=[
            jax.ShapeDtypeStruct(queries.shape, bf16),
            jax.ShapeDtypeStruct((groups, REP, tokens), f32),
        ],
        cost_estimate=estimate(
            pairs * REP * chunk * chunk * HD * 4 * 2,
            queries.size * 4 + keys.size * 4,
            pairs * REP * chunk * chunk,
        ),
        name="attention_forward",
    )(qpos, kpos, lengths, queries, keys, values)


def attention_bwd_body(
    chunk, blocks, qpos_ref, kpos_ref, len_ref, q_ref, k_ref, v_ref, o_ref, do_ref, lse_ref,
    dq_ref, dk_ref, dv_ref, kn_ref, vn_ref, dqa_ref, dka_ref, dva_ref, delta_ref,
):
    s, qb = pl.program_id(0), pl.program_id(2)
    ys = k_ref.shape[0]

    @pl.when(qb == 0)
    def _():
        dka_ref[...] = jnp.zeros_like(dka_ref)
        dva_ref[...] = jnp.zeros_like(dva_ref)
        for yk in range(ys):
            for b in range(blocks):
                rows = pl.ds((yk * blocks + b) * chunk, chunk)
                cols = pl.ds(b * chunk, chunk)
                kn_ref[rows, :] = k_ref[yk, :, cols].astype(f32).T.astype(bf16)
                vn_ref[rows, :] = v_ref[yk, :, cols].astype(f32).T.astype(bf16)

    qp = qpos_ref[s, qb]
    length = len_ref[s]
    dqa_ref[...] = jnp.zeros_like(dqa_ref)
    for h in range(REP):
        rows = slice(h * HD, (h + 1) * HD)
        delta_ref[h : h + 1, :] = jnp.sum(
            do_ref[rows, :].astype(f32) * o_ref[rows, :].astype(f32), axis=0, keepdims=True
        )

    for yk in range(ys):

        def step(b, carry, yk=yk):
            kp = kpos_ref[s, yk * blocks + b]
            first = kp * chunk
            live = (kp <= qp) & (first < length)
            partly = (kp == qp) | (first + chunk > length)

            def work(masked):
                at = pl.ds(pl.multiple_of((yk * blocks + b) * chunk, chunk), chunk)
                cols = pl.ds(pl.multiple_of(b * chunk, chunk), chunk)
                kn, vn = kn_ref[at, :], vn_ref[at, :]
                kt = k_ref[yk, :, cols]
                if masked:
                    at_key = first + lax.broadcasted_iota(jnp.int32, (chunk, chunk), 0)
                    at_query = qp * chunk + lax.broadcasted_iota(jnp.int32, (chunk, chunk), 1)
                    allowed = (at_key <= at_query) & (at_key < length)
                dk = dka_ref[yk, :, cols]
                dv = dva_ref[yk, :, cols]
                for h in range(REP):
                    rows = slice(h * HD, (h + 1) * HD)
                    qt, dot = q_ref[rows, :], do_ref[rows, :]
                    scores = jnp.dot(kn, qt, preferred_element_type=f32)
                    if masked:
                        scores = jnp.where(allowed, scores, masked_score)
                    probs = jnp.exp(scores - lse_ref[0, h : h + 1, :])
                    grad_probs = jnp.dot(vn, dot, preferred_element_type=f32)
                    grad_scores = (probs * (grad_probs - delta_ref[h : h + 1, :])).astype(bf16)
                    dqa_ref[rows, :] += jnp.dot(kt, grad_scores, preferred_element_type=f32)
                    dk += lax.dot_general(
                        qt, grad_scores, (((1,), (1,)), ((), ())), preferred_element_type=f32
                    )
                    dv += lax.dot_general(
                        dot, probs.astype(bf16), (((1,), (1,)), ((), ())),
                        preferred_element_type=f32,
                    )
                dka_ref[yk, :, cols] = dk
                dva_ref[yk, :, cols] = dv

            pl.when(live & partly)(lambda: work(True))
            pl.when(live & jnp.logical_not(partly))(lambda: work(False))
            return carry

        lax.fori_loop(0, blocks, step, 0)

    dq_ref[...] = dqa_ref[...] * 0.125

    @pl.when(qb == blocks - 1)
    def _():
        dk_ref[...] = dka_ref[...].astype(bf16)
        dv_ref[...] = dva_ref[...].astype(bf16)


def attention_bwd(queries, keys, values, attended, grads, lse, qpos, kpos, lengths, chunk):
    tokens = queries.shape[1]
    groups = queries.shape[0] // (REP * HD)
    ys = keys.shape[0]
    half = tokens // 2
    blocks = half // chunk
    q_spec = pl.BlockSpec((REP * HD, chunk), lambda s, g, b, *_: (g, s * blocks + b))
    kv_spec = pl.BlockSpec((ys, HD, half), lambda s, g, b, *_: (0, g, s))
    lse_spec = pl.BlockSpec((1, REP, chunk), lambda s, g, b, *_: (g, 0, s * blocks + b))
    pairs = 2 * groups * blocks * blocks * ys
    return pl.pallas_call(
        functools.partial(attention_bwd_body, chunk, blocks),
        grid_spec=pltpu.PrefetchScalarGridSpec(
            num_scalar_prefetch=3,
            grid=(2, groups, blocks),
            in_specs=[q_spec, kv_spec, kv_spec, q_spec, q_spec, lse_spec],
            out_specs=[q_spec, kv_spec, kv_spec],
            scratch_shapes=[
                pltpu.VMEM((ys * half, HD), bf16),
                pltpu.VMEM((ys * half, HD), bf16),
                pltpu.VMEM((REP * HD, chunk), f32),
                pltpu.VMEM((ys, HD, half), f32),
                pltpu.VMEM((ys, HD, half), f32),
                pltpu.VMEM((8, chunk), f32),
            ],
        ),
        out_shape=[
            jax.ShapeDtypeStruct(queries.shape, f32),
            jax.ShapeDtypeStruct(keys.shape, bf16),
            jax.ShapeDtypeStruct(keys.shape, bf16),
        ],
        cost_estimate=estimate(
            pairs * REP * chunk * chunk * HD * 10 * 2,
            queries.size * 10 + keys.size * 8,
            pairs * REP * chunk * chunk,
        ),
        name="attention_backward",
    )(qpos, kpos, lengths, queries, keys, values, attended, grads, lse)


def rotate(vectors, cos_table, sin_table, back=False):
    heads = vectors.shape[0] // HD
    halves = vectors.reshape(heads, 2, HD // 2, vectors.shape[1])
    a, b = halves[:, 0], halves[:, 1]
    sin_table = -sin_table if back else sin_table
    turned = jnp.stack([a * cos_table - b * sin_table, b * cos_table + a * sin_table], axis=1)
    return turned.reshape(vectors.shape)


def contract(left, right, left_dim, right_dim):
    return lax.dot_general(
        left, right, (((left_dim,), (right_dim,)), ((), ())), preferred_element_type=f32
    )


def body(
    tokens_in, grad_out, seq_lengths, stretch_order, attn_gain, query_w, key_w, value_w,
    output_w, mlp_gain, gate_w, up_w, down_w,
):
    zs, ys = lax.axis_size("z"), lax.axis_size("y")
    z, c, y, x = (lax.axis_index(name) for name in ("z", "c", "y", "x"))
    rows, width = tokens_in.shape[1:]
    chunk = rows // 2
    unit = width // (zs * ys)

    def to_slots(value):
        if (unit // 2) % 128 == 0:
            return move_columns(value, y[None], zs, ys, True)
        parts = value.reshape(value.shape[0], zs, 2, ys, unit // 2)
        parts = [lax.dynamic_index_in_dim(parts, (y - k) % ys, 3) for k in range(ys)]
        return jnp.concatenate(
            [jnp.transpose(p, (0, 3, 1, 2, 4)).reshape(value.shape[0], width // ys) for p in parts],
            axis=1,
        )

    def from_slots(value):
        if (unit // 2) % 128 == 0:
            return move_columns(value, y[None], zs, ys, False)
        parts = value.reshape(value.shape[0], ys, zs, 2, unit // 2)
        parts = jnp.stack(
            [lax.dynamic_index_in_dim(parts, (y - k) % ys, 1, keepdims=False) for k in range(ys)], axis=3
        )
        return parts.reshape(value.shape[0], width)

    orders = jnp.stack([stretch_order[0], shift(stretch_order[0], "c", 1)])
    lengths = jnp.concatenate([seq_lengths, shift(seq_lengths, "c", 1)])
    slots = [
        2 * (((y - k) % ys) * 2 + (x if i == 0 else 1 - x)) + b
        for k in range(ys)
        for i in range(2)
        for b in range(2)
    ]
    kpos = jnp.stack([lax.dynamic_index_in_dim(orders, s, 1, keepdims=False) for s in slots], axis=1)
    qpos = kpos[:, :4]
    token_pos = (qpos[:, :, None] * chunk + jnp.arange(chunk, dtype=jnp.int32)).reshape(4 * rows)
    own_pos = token_pos[:rows]
    live = (own_pos < seq_lengths[0]).astype(f32)[:, None]
    angles = frequencies()[:, None] * token_pos.astype(f32)[None, :]
    cos_table, sin_table = jnp.cos(angles), jnp.sin(angles)

    gains = jnp.stack([attn_gain, mlp_gain])
    gains = in_order(gains, shift(gains, "x", 1), x, 1)
    gains = in_order(gains, shift(gains, "c", 1), c, 1)
    gains = gather_gains(gains).astype(f32)
    gain_one, gain_two = gains[0:1], gains[1:2]

    inputs = to_slots(tokens_in[0]).astype(f32)
    scale_one = lax.rsqrt(jnp.mean(inputs * inputs, axis=1, keepdims=True) + epsilon)
    unit_one = inputs * scale_one
    normed_own = (unit_one * gain_one).astype(bf16)

    def packed(*weights):
        return jnp.concatenate(
            [w[:, t * (w.shape[1] // 4) : (t + 1) * (w.shape[1] // 4)] for t in range(4) for w in weights],
            axis=1,
        )

    nq, nk = query_w.shape[1] // 4, key_w.shape[1] // 4
    nqkv = nq + 2 * nk
    attn_unit = spread_columns(packed(query_w, key_w, value_w, output_w), c, x)
    qkv_unit, out_unit = attn_unit[:, :nqkv], attn_unit[:, nqkv:]
    mlp_unit = spread_columns(packed(gate_w, up_w, down_w), c, x, (attn_unit,), (normed_own,))
    nf = gate_w.shape[1] // 4
    gate_unit, up_unit, down_unit = (mlp_unit[:, i * nf : (i + 1) * nf] for i in range(3))
    qkv_slots = gather_slots(gather_column(qkv_unit))
    out_column = hold(gather_column(hold(out_unit, qkv_unit)), *qkv_slots[1:])
    qkv_w = jnp.concatenate(qkv_slots, axis=0)
    out_w = jnp.concatenate(gather_slots(out_column), axis=0)
    gate_column = gather_column(hold(gate_unit, out_column))
    up_all, down_all = gather_whole(up_unit, y), gather_whole(down_unit, y)

    normed_one = gather_tokens(normed_own, *qkv_slots[1:])
    pre = contract(after(qkv_w, mlp_unit), normed_one, 0, 1)
    queries = (rotate(pre[:nq], cos_table, sin_table).astype(bf16)) * jnp.asarray(0.125, bf16)
    key_own = rotate(pre[nq : nq + nk], cos_table, sin_table).astype(bf16)
    value_own = pre[nq + nk :].astype(bf16)
    both_own = jnp.concatenate([key_own, value_own], axis=0)
    both = jnp.stack([both_own] + [shift(both_own, "y", k) for k in range(1, ys)])
    keys, values = both[:, :nk], both[:, nk:]
    gate_all = gather_slots(hold(gate_column, both))
    grad_own = to_slots(grad_out[0]) * live.astype(bf16)
    grad_rows = grad_own.astype(f32)
    grad_low = gather_tokens(after(grad_own, normed_one))
    attended, lse = attention_fwd(after(queries, grad_own, gate_all[0]), keys, values, qpos, kpos, lengths, chunk)
    middle = inputs + scatter_tokens([contract(after(attended, grad_low, *gate_all[1:]), out_w, 0, 1).astype(bf16)])
    scale_two = lax.rsqrt(jnp.mean(middle * middle, axis=1, keepdims=True) + epsilon)
    unit_two = middle * scale_two
    normed_two = gather_tokens((unit_two * gain_two).astype(bf16))

    (gate_pre,) = rows_product(normed_two, gate_all, [], plain, 1, "gate")
    up_pre, hidden = rows_product(normed_two, up_all, [gate_pre], up_finish, 2, "up")

    def finish(total):
        return join_columns(total, c, x)

    by_y = (y - jnp.arange(ys, dtype=jnp.int32)) % ys
    last = columns_product(grad_low, by_y, ys, hidden, [], "down_grad")
    down_grad = scatter_whole(last)
    grad_gate, grad_up = rows_product(
        after(grad_low, last), down_all, [gate_pre, up_pre], hidden_back, 2, "hidden_grad"
    )
    last = columns_product(normed_two, by_y, ys, grad_gate, [], "gate_grad")
    gate_grad = scatter_whole(last)
    last = columns_product(after(normed_two, last), by_y, ys, grad_up, [], "up_grad")
    up_grad = scatter_whole(last)
    norm_parts = []
    for g, u in zip(gate_all, up_all):
        last = turned_product([after(grad_gate, last), grad_up], [g, u], "norm_grad")
        norm_parts.append(last)
    grad_norm_two = scatter_tokens(norm_parts)
    branch_parts = []
    for w in down_all:
        last = turned_product([after(hidden, last)], [w], "down")
        branch_parts.append(last)
    gain_two_grad = jnp.sum(grad_norm_two * unit_two, axis=0)
    def gain_back(terms):
        own, other = halves(scatter_gains(terms, unit), c, 0)
        own, other = halves(own + shift(other, "c", 1), x, 0)
        return own + shift(other, "x", 1)

    scaled_two = grad_norm_two * gain_two
    grad_middle = grad_rows + scale_two * (
        scaled_two - unit_two * jnp.mean(scaled_two * unit_two, axis=1, keepdims=True)
    )

    def attn_terms(activations, grads, k):
        size = width // ys
        return contract(lax.dynamic_slice_in_dim(activations, k * size, size, 1), grads, 0, 1)

    grad_branch = gather_tokens(grad_middle.astype(bf16))
    branch_two = scatter_tokens([after(part, grad_branch) for part in branch_parts])
    result = from_slots(((middle + branch_two) * live).astype(bf16))[None]
    grad_attn = contract(out_w, after(grad_branch, last), 0, 1).astype(bf16)
    output_grad = scatter_whole(
        jnp.concatenate([attn_terms(grad_branch, attended, by_y[i]) for i in range(ys)], axis=0).astype(bf16)
    )
    grad_query, grad_keys, grad_values = attention_bwd(
        after(queries, down_grad), keys, values, attended, grad_attn, lse, qpos, kpos, lengths, chunk
    )
    gain_two_back = gain_back(hold(gain_two_grad, grad_query))
    grad_both = jnp.concatenate([grad_keys, grad_values], axis=1)
    grad_both = sum(
        [grad_both[0].astype(f32)]
        + [shift(grad_both[k], "y", -k).astype(f32) for k in range(1, ys)]
    )
    grad_qkv = jnp.concatenate(
        [
            rotate(grad_query, cos_table, sin_table, True).astype(bf16),
            rotate(grad_both[:nk], cos_table, sin_table, True).astype(bf16),
            grad_both[nk:].astype(bf16),
        ],
        axis=0,
    )
    qkv_sent = send_slots([attn_terms(normed_one, grad_qkv, k).astype(bf16) for k in range(1, ys)])
    down_grad = finish(down_grad)
    gate_grad = finish(after(gate_grad, grad_query))
    grad_norm_one = scatter_tokens(
        [contract(after(grad_qkv, down_grad, gate_grad, result), qkv_w, 0, 1).astype(bf16)]
    )
    qkv_grad = sum([attn_terms(normed_one, grad_qkv, 0)] + [t.astype(f32) for t in qkv_sent])
    qkv_grad = scatter_column(qkv_grad.astype(bf16))
    gain_one_grad = jnp.sum(grad_norm_one * unit_one, axis=0)
    scaled_one = grad_norm_one * gain_one
    up_grad = finish(up_grad)
    scaled_one = after(scaled_one, up_grad)
    grad_inputs = grad_middle + scale_one * (
        scaled_one - unit_one * jnp.mean(scaled_one * unit_one, axis=1, keepdims=True)
    )

    qkv_back = finish(qkv_grad)

    def columns(low, high):
        return jnp.concatenate(
            [qkv_back[:, t * nqkv + low : t * nqkv + high] for t in range(4)], axis=1
        ).astype(f32)

    return (
        result,
        from_slots(grad_inputs)[None],
        gain_back(gain_one_grad),
        columns(0, nq),
        columns(nq, nq + nk),
        columns(nq + nk, nqkv),
        finish(output_grad).astype(f32),
        gain_two_back,
        gate_grad.astype(f32),
        up_grad.astype(f32),
        down_grad.astype(f32),
    )


def solution(mesh):
    dp, seq = mesh.shape["dp"], mesh.shape["seq"]
    fine = Mesh(mesh.devices.reshape(dp // 2, 2, seq // 2, 2), ("z", "c", "y", "x"))
    every = ("z", "c", "y", "x")
    tokens = P(("z", "c"), ("y", "x"), None)
    vector, matrix = P(every), P(every, None)
    return jax.shard_map(
        body,
        mesh=fine,
        in_specs=(
            tokens, tokens, P(("z", "c")), P(("z", "c"), None), vector, matrix, matrix, matrix,
            matrix, vector, matrix, matrix, matrix,
        ),
        out_specs=(
            tokens, tokens, vector, matrix, matrix, matrix, matrix, vector, matrix, matrix, matrix,
        ),
        check_vma=False,
    )
```

```python
import functools
import math

import jax
import jax.numpy as jnp
from jax import lax
from jax.experimental import pallas as pl
from jax.experimental.pallas import tpu as pltpu
from jax.sharding import Mesh
from jax.sharding import PartitionSpec as P

HEADS = 32
KVH = 8
HD = 64
REP = HEADS // KVH

epsilon = 1e-05
masked_score = -1e30
floor_score = -1e29

bf16 = jnp.bfloat16
f32 = jnp.float32


def frequencies():
    steps_even = jnp.arange(0, HD, 2).astype(f32) / HD
    base_freq = 1.0 / 500000.0**steps_even
    wavelength = 2.0 * math.pi / base_freq
    smooth = (8192.0 / wavelength - 1.0) / 3.0
    blended = (1.0 - smooth) * base_freq / 32.0 + smooth * base_freq
    return jnp.where(
        wavelength < 2048.0, base_freq, jnp.where(wavelength > 8192.0, base_freq / 32.0, blended)
    )


def shift(value, axis, steps):
    size = lax.axis_size(axis)
    return lax.ppermute(value, axis, [(i, (i + steps) % size) for i in range(size)])


def in_order(own, other, index, axis):
    return jnp.where(
        index == 0,
        jnp.concatenate([own, other], axis=axis),
        jnp.concatenate([other, own], axis=axis),
    )


def halves(value, index, axis):
    size = value.shape[axis] // 2
    return (
        lax.dynamic_slice_in_dim(value, index * size, size, axis),
        lax.dynamic_slice_in_dim(value, (1 - index) * size, size, axis),
    )


def spread_columns(shard, c, x, earlier=(), later=()):
    own, other = halves(shard, x, 1)
    if earlier:
        other = hold(other, *earlier)
    both = in_order(own, after(shift(other, "x", 1), *later), x, 0)
    own, other = halves(both, c, 1)
    return in_order(own, shift(other, "c", 1), c, 0)


def join_by_c(unit, c):
    own, other = halves(unit, c, 0)
    return own, shift(other, "c", 1)


def join_by_x(own, got, c, x):
    own, other = halves(in_order(own, got, c, 1), x, 0)
    return own, shift(other, "x", 1)


def join_columns(unit, c, x):
    own, got = join_by_x(*join_by_c(unit, c), c, x)
    return in_order(own, got, x, 1)


def after(value, *others):
    return lax.optimization_barrier((value,) + others)[0]


def hold_body(*refs):
    del refs


def hold(value, *others):
    return pl.pallas_call(
        hold_body,
        in_specs=[pl.BlockSpec(memory_space=pl.ANY)] * (1 + len(others)),
        out_specs=pl.BlockSpec(memory_space=pl.ANY),
        out_shape=jax.ShapeDtypeStruct(value.shape, value.dtype),
        input_output_aliases={0: 0},
        name="hold",
    )(value, *others)


def gather_column(unit):
    return lax.all_gather(unit, "z", axis=0, tiled=True)


def gather_slots(column):
    return [column] + [shift(column, "y", k) for k in range(1, lax.axis_size("y"))]


def send_slots(terms):
    return [shift(term, "y", -(k + 1)) for k, term in enumerate(terms)]


def gather_whole(unit, y):
    zs, ys = lax.axis_size("z"), lax.axis_size("y")
    size = zs * unit.shape[0]
    whole = lax.all_gather(unit, ("y", "z"), axis=0, tiled=True)
    return [lax.dynamic_slice_in_dim(whole, ((y - k) % ys) * size, size, 0) for k in range(ys)]


def scatter_whole(terms):
    return lax.psum_scatter(terms, ("y", "z"), scatter_dimension=0, tiled=True)


def scatter_column(total):
    return lax.psum_scatter(total, "z", scatter_dimension=0, tiled=True)


def gather_gains(unit):
    zs, ys = lax.axis_size("z"), lax.axis_size("y")
    row = jnp.stack([unit] + [shift(unit, "y", k) for k in range(1, ys)], axis=1)
    z = lax.axis_index("z")
    out = jnp.zeros((2, ys, zs, unit.shape[1]), unit.dtype)
    for j in range(zs):
        got = row if j == 0 else shift(row, "z", j)
        out = lax.dynamic_update_slice(out, got[:, :, None], (0, 0, (z - j) % zs, 0))
    return out.reshape(2, -1)


def scatter_gains(terms, unit):
    zs, ys = lax.axis_size("z"), lax.axis_size("y")
    z = lax.axis_index("z")
    terms = terms.reshape(ys, zs * unit)
    total = terms[0]
    for k in range(1, ys):
        total = total + shift(terms[k], "y", -k)
    total = total.reshape(zs, unit)
    out = lax.dynamic_index_in_dim(total, z, 0, keepdims=False)
    for j in range(1, zs):
        out = out + shift(lax.dynamic_index_in_dim(total, (z - j) % zs, 0, keepdims=False), "z", -j)
    return out


def group_tokens(own):
    beside = shift(own, "x", 1)
    return own, beside, shift(own, "c", 1), shift(beside, "c", 1)


def scatter_by_c(partial, by_sequence):
    count = partial.shape[0] // 4
    mine = partial[:count]
    if by_sequence:
        beside, sent = partial[count : 2 * count], partial[2 * count :]
    else:
        beside, sent = partial[3 * count :], partial[count : 3 * count]
    got = shift(sent, "c", 1).astype(f32)
    return mine.astype(f32) + got[:count], beside.astype(f32) + got[count:]


def scatter_tokens(partials, by_sequence):
    sums = []
    for partial in partials:
        mine, beside = scatter_by_c(partial, by_sequence)
        sums.append(mine + shift(beside.astype(bf16), "x", 1).astype(f32))
    return jnp.concatenate(sums, axis=1)


def move_columns_body(zs, ys, forth, y_ref, in_ref, out_ref):
    block = in_ref.shape[1] // (zs * 2 * ys)
    y = y_ref[0]
    for i in range(zs * 2):
        for k in range(ys):
            natural = i * ys + lax.rem(y - k + ys, ys)
            natural = pl.ds(pl.multiple_of(natural * block, block), block)
            slot = pl.ds((k * zs * 2 + i) * block, block)
            if forth:
                out_ref[:, slot] = in_ref[:, natural]
            else:
                out_ref[:, natural] = in_ref[:, slot]


def move_columns(value, y, zs, ys, forth):
    rows, width = value.shape
    tall = rows // 4
    spec = pl.BlockSpec((tall, width), lambda i, *_: (i, 0))
    return pl.pallas_call(
        functools.partial(move_columns_body, zs, ys, forth),
        grid_spec=pltpu.PrefetchScalarGridSpec(
            num_scalar_prefetch=1, grid=(4,), in_specs=[spec], out_specs=spec
        ),
        out_shape=jax.ShapeDtypeStruct(value.shape, value.dtype),
        cost_estimate=pl.CostEstimate(
            flops=0, bytes_accessed=2 * value.size * value.dtype.itemsize, transcendentals=0
        ),
        name="move_columns",
    )(y, value)


VMEM_BYTES = 56 * 1024 * 1024
EASE = 1


def estimate(flops, moved, exps=0):
    return pl.CostEstimate(
        flops=int(flops) // EASE, bytes_accessed=int(moved) // EASE, transcendentals=int(exps) // EASE
    )


def fit(size, most):
    return size if size <= most else fit(size // 2, most)


def rows_product(left, parts, extras, finish, n_out, name):
    t, d = left.shape
    n = parts[0].shape[1]
    depth = parts[0].shape[0]
    bm, bn = fit(t, 512), fit(n, 1024)
    n_parts, n_extra = len(parts), len(extras)

    def kernel(*refs):
        left_ref = refs[0]
        product = None
        for p in range(n_parts):
            term = jnp.dot(
                left_ref[:, p * depth : (p + 1) * depth], refs[1 + p][...], preferred_element_type=f32
            )
            product = term if product is None else product + term
        got = finish(product, *(r[...] for r in refs[1 + n_parts : 1 + n_parts + n_extra]))
        for ref, value in zip(refs[1 + n_parts + n_extra :], got):
            ref[...] = value.astype(bf16)

    tile = pl.BlockSpec((bm, bn), lambda j, i: (i, j))
    return pl.pallas_call(
        kernel,
        grid=(n // bn, t // bm),
        in_specs=[pl.BlockSpec((bm, d), lambda j, i: (i, 0))]
        + [pl.BlockSpec((depth, bn), lambda j, i: (0, j))] * n_parts
        + [tile] * n_extra,
        out_specs=[tile] * n_out,
        out_shape=[jax.ShapeDtypeStruct((t, n), bf16)] * n_out,
        compiler_params=pltpu.CompilerParams(vmem_limit_bytes=VMEM_BYTES),
        cost_estimate=estimate(2 * t * d * n, 2 * (t * d + d * n + t * n)),
        name=name,
    )(left, *parts, *extras)


def turned_product(lefts, rights, name):
    t, f = lefts[0].shape
    n = rights[0].shape[0]
    bm, bn = fit(t, 512), fit(n, 1024)
    count = len(lefts)

    def kernel(*refs):
        product = None
        for p in range(count):
            term = lax.dot_general(
                refs[p][...], refs[count + p][...], (((1,), (1,)), ((), ())), preferred_element_type=f32
            )
            product = term if product is None else product + term
        refs[2 * count][...] = product.astype(bf16)

    return pl.pallas_call(
        kernel,
        grid=(n // bn, t // bm),
        in_specs=[pl.BlockSpec((bm, f), lambda j, i: (i, 0))] * count
        + [pl.BlockSpec((bn, f), lambda j, i: (j, 0))] * count,
        out_specs=pl.BlockSpec((bm, bn), lambda j, i: (i, j)),
        out_shape=jax.ShapeDtypeStruct((t, n), bf16),
        compiler_params=pltpu.CompilerParams(vmem_limit_bytes=VMEM_BYTES),
        cost_estimate=estimate(2 * count * t * f * n, 2 * count * (t * f + f * n)),
        name=name,
    )(*lefts, *rights)


def columns_product(left, slots, n_parts, right, others, name):
    t, d = left.shape
    m = d // n_parts
    f = right.shape[1]
    bm, bn = fit(m, 512), fit(f, 1024)
    per = m // bm
    count = len(others)

    def kernel(slots_ref, left_ref, right_ref, *refs):
        turned_ref = refs[-1]

        @pl.when(pl.program_id(1) == 0)
        def _():
            turned_ref[...] = left_ref[...].T

        product = jnp.dot(turned_ref[...], right_ref[...], preferred_element_type=f32)
        for ref in refs[:count]:
            product = product + ref[...].astype(f32)
        refs[count][...] = product.astype(bf16)

    rows = slots.shape[0] * m
    tile = pl.BlockSpec((bm, bn), lambda i, j, slots_ref: (i, j))
    return pl.pallas_call(
        kernel,
        grid_spec=pltpu.PrefetchScalarGridSpec(
            num_scalar_prefetch=1,
            grid=(rows // bm, f // bn),
            in_specs=[
                pl.BlockSpec((t, bm), lambda i, j, slots_ref: (0, slots_ref[i // per] * per + i % per)),
                pl.BlockSpec((t, bn), lambda i, j, slots_ref: (0, j)),
            ]
            + [tile] * count,
            out_specs=tile,
            scratch_shapes=[pltpu.VMEM((bm, t), bf16)],
        ),
        out_shape=jax.ShapeDtypeStruct((rows, f), bf16),
        compiler_params=pltpu.CompilerParams(vmem_limit_bytes=VMEM_BYTES),
        cost_estimate=estimate(2 * t * rows * f, 2 * (t * m + t * f + rows * f)),
        name=name,
    )(slots, left, right, *others)


def plain(product):
    return (product,)


def up_finish(product, gate):
    gate = gate.astype(f32)
    return product, gate * jax.nn.sigmoid(gate) * product


def hidden_back(grad, gate, up):
    gate, up = gate.astype(f32), up.astype(f32)
    sigmoid = jax.nn.sigmoid(gate)
    return grad * up * sigmoid * (1.0 + gate * (1.0 - sigmoid)), grad * gate * sigmoid


def attention_fwd_body(
    chunk, blocks, part, qpos_ref, kpos_ref, len_ref, q_ref, k_ref, v_ref, o_ref, lse_ref,
    kn_ref, m_ref, l_ref, acc_ref,
):
    s, qb = pl.program_id(0), pl.program_id(2)
    ys = k_ref.shape[0]

    @pl.when(qb == 0)
    def _():
        for yk in range(ys):
            for b in range(blocks):
                kn_ref[pl.ds((yk * blocks + b) * chunk, chunk), :] = (
                    k_ref[yk, :, pl.ds(b * chunk, chunk)].astype(f32).T.astype(bf16)
                )

    qp = qpos_ref[s, part * (blocks // 2) + qb]
    length = len_ref[s]
    m_ref[...] = jnp.full_like(m_ref, floor_score)
    l_ref[...] = jnp.zeros_like(l_ref)
    acc_ref[...] = jnp.zeros_like(acc_ref)

    for yk in range(ys):

        def step(b, carry, yk=yk):
            kp = kpos_ref[s, yk * blocks + b]
            first = kp * chunk
            live = (kp <= qp) & (first < length)
            partly = (kp == qp) | (first + chunk > length)

            def work(masked):
                kn = kn_ref[pl.ds(pl.multiple_of((yk * blocks + b) * chunk, chunk), chunk), :]
                vt = v_ref[yk, :, pl.ds(pl.multiple_of(b * chunk, chunk), chunk)]
                if masked:
                    at_key = first + lax.broadcasted_iota(jnp.int32, (chunk, chunk), 0)
                    at_query = qp * chunk + lax.broadcasted_iota(jnp.int32, (chunk, chunk), 1)
                    allowed = (at_key <= at_query) & (at_key < length)
                for h in range(REP):
                    rows = slice(h * HD, (h + 1) * HD)
                    scores = jnp.dot(kn, q_ref[rows, :], preferred_element_type=f32)
                    if masked:
                        scores = jnp.where(allowed, scores, masked_score)
                    m_old = m_ref[h : h + 1, :]
                    m_new = jnp.maximum(m_old, jnp.max(scores, axis=0, keepdims=True))
                    alpha = jnp.exp(m_old - m_new)
                    probs = jnp.exp(scores - m_new)
                    m_ref[h : h + 1, :] = m_new
                    l_ref[h : h + 1, :] = l_ref[h : h + 1, :] * alpha + jnp.sum(
                        probs, axis=0, keepdims=True
                    )
                    acc_ref[rows, :] = acc_ref[rows, :] * alpha + jnp.dot(
                        vt, probs.astype(bf16), preferred_element_type=f32
                    )

            pl.when(live & partly)(lambda: work(True))
            pl.when(live & jnp.logical_not(partly))(lambda: work(False))
            return carry

        lax.fori_loop(0, blocks, step, 0)

    for h in range(REP):
        rows = slice(h * HD, (h + 1) * HD)
        o_ref[rows, :] = (acc_ref[rows, :] / l_ref[h : h + 1, :]).astype(bf16)
    lse_ref[0] = m_ref[0:REP, :] + jnp.log(l_ref[0:REP, :])


def attention_fwd(queries, keys, values, qpos, kpos, lengths, chunk, part):
    tokens = queries.shape[1]
    groups = queries.shape[0] // (REP * HD)
    ys = keys.shape[0]
    half = tokens // 2
    blocks = half // chunk
    few = blocks // 2
    q_spec = pl.BlockSpec((REP * HD, chunk), lambda s, g, b, *_: (g, s * blocks + part * few + b))
    o_spec = pl.BlockSpec((REP * HD, chunk), lambda s, g, b, *_: (g, ((s + part) % 2) * few + b))
    kv_spec = pl.BlockSpec((ys, HD, half), lambda s, g, b, *_: (0, g, s))
    lse_spec = pl.BlockSpec((1, REP, chunk), lambda s, g, b, *_: (g, 0, ((s + part) % 2) * few + b))
    pairs = 2 * groups * few * blocks * ys
    return pl.pallas_call(
        functools.partial(attention_fwd_body, chunk, blocks, part),
        grid_spec=pltpu.PrefetchScalarGridSpec(
            num_scalar_prefetch=3,
            grid=(2, groups, few),
            in_specs=[q_spec, kv_spec, kv_spec],
            out_specs=[o_spec, lse_spec],
            scratch_shapes=[
                pltpu.VMEM((ys * half, HD), bf16),
                pltpu.VMEM((8, chunk), f32),
                pltpu.VMEM((8, chunk), f32),
                pltpu.VMEM((REP * HD, chunk), f32),
            ],
        ),
        out_shape=[
            jax.ShapeDtypeStruct((queries.shape[0], half), bf16),
            jax.ShapeDtypeStruct((groups, REP, half), f32),
        ],
        cost_estimate=estimate(
            pairs * REP * chunk * chunk * HD * 4 * 8,
            queries.size * 2 + keys.size * 4,
            pairs * REP * chunk * chunk,
        ),
        name="attention_forward",
    )(qpos, kpos, lengths, queries, keys, values)


def attention_bwd_body(
    chunk, blocks, part, n_before, qpos_ref, kpos_ref, len_ref, q_ref, k_ref, v_ref, o_ref, do_ref,
    lse_ref, *refs,
):
    before = refs[:n_before]
    dq_ref, dk_ref, dv_ref, kn_ref, vn_ref, dqa_ref, dka_ref, dva_ref, delta_ref = refs[n_before:]
    s, qb = pl.program_id(0), pl.program_id(2)
    ys = k_ref.shape[0]

    @pl.when(qb == 0)
    def _():
        if before:
            dka_ref[...] = before[0][...]
            dva_ref[...] = before[1][...]
        else:
            dka_ref[...] = jnp.zeros_like(dka_ref)
            dva_ref[...] = jnp.zeros_like(dva_ref)
        for yk in range(ys):
            for b in range(blocks):
                rows = pl.ds((yk * blocks + b) * chunk, chunk)
                cols = pl.ds(b * chunk, chunk)
                kn_ref[rows, :] = k_ref[yk, :, cols].astype(f32).T.astype(bf16)
                vn_ref[rows, :] = v_ref[yk, :, cols].astype(f32).T.astype(bf16)

    qp = qpos_ref[s, part * (blocks // 2) + qb]
    length = len_ref[s]
    dqa_ref[...] = jnp.zeros_like(dqa_ref)
    for h in range(REP):
        rows = slice(h * HD, (h + 1) * HD)
        delta_ref[h : h + 1, :] = jnp.sum(
            do_ref[rows, :].astype(f32) * o_ref[rows, :].astype(f32), axis=0, keepdims=True
        )

    for yk in range(ys):

        def step(b, carry, yk=yk):
            kp = kpos_ref[s, yk * blocks + b]
            first = kp * chunk
            live = (kp <= qp) & (first < length)
            partly = (kp == qp) | (first + chunk > length)

            def work(masked):
                at = pl.ds(pl.multiple_of((yk * blocks + b) * chunk, chunk), chunk)
                cols = pl.ds(pl.multiple_of(b * chunk, chunk), chunk)
                kn, vn = kn_ref[at, :], vn_ref[at, :]
                kt = k_ref[yk, :, cols]
                if masked:
                    at_key = first + lax.broadcasted_iota(jnp.int32, (chunk, chunk), 0)
                    at_query = qp * chunk + lax.broadcasted_iota(jnp.int32, (chunk, chunk), 1)
                    allowed = (at_key <= at_query) & (at_key < length)
                dk = dka_ref[yk, :, cols]
                dv = dva_ref[yk, :, cols]
                for h in range(REP):
                    rows = slice(h * HD, (h + 1) * HD)
                    qt, dot = q_ref[rows, :], do_ref[rows, :]
                    scores = jnp.dot(kn, qt, preferred_element_type=f32)
                    if masked:
                        scores = jnp.where(allowed, scores, masked_score)
                    probs = jnp.exp(scores - lse_ref[0, h : h + 1, :])
                    grad_probs = jnp.dot(vn, dot, preferred_element_type=f32)
                    grad_scores = (probs * (grad_probs - delta_ref[h : h + 1, :])).astype(bf16)
                    dqa_ref[rows, :] += jnp.dot(kt, grad_scores, preferred_element_type=f32)
                    dk += lax.dot_general(
                        qt, grad_scores, (((1,), (1,)), ((), ())), preferred_element_type=f32
                    )
                    dv += lax.dot_general(
                        dot, probs.astype(bf16), (((1,), (1,)), ((), ())),
                        preferred_element_type=f32,
                    )
                dka_ref[yk, :, cols] = dk
                dva_ref[yk, :, cols] = dv

            pl.when(live & partly)(lambda: work(True))
            pl.when(live & jnp.logical_not(partly))(lambda: work(False))
            return carry

        lax.fori_loop(0, blocks, step, 0)

    dq_ref[...] = dqa_ref[...] * 0.125

    @pl.when(qb == blocks // 2 - 1)
    def _():
        dk_ref[...] = dka_ref[...].astype(dk_ref.dtype)
        dv_ref[...] = dva_ref[...].astype(dv_ref.dtype)


def attention_bwd(queries, keys, values, attended, grads, lse, qpos, kpos, lengths, chunk, part, *before):
    tokens = queries.shape[1]
    groups = queries.shape[0] // (REP * HD)
    ys = keys.shape[0]
    half = tokens // 2
    blocks = half // chunk
    few = blocks // 2
    q_spec = pl.BlockSpec((REP * HD, chunk), lambda s, g, b, *_: (g, s * blocks + part * few + b))
    o_spec = pl.BlockSpec((REP * HD, chunk), lambda s, g, b, *_: (g, ((s + part) % 2) * few + b))
    kv_spec = pl.BlockSpec((ys, HD, half), lambda s, g, b, *_: (0, g, s))
    lse_spec = pl.BlockSpec((1, REP, chunk), lambda s, g, b, *_: (g, 0, ((s + part) % 2) * few + b))
    pairs = 2 * groups * few * blocks * ys
    kind = bf16 if before else f32
    return pl.pallas_call(
        functools.partial(attention_bwd_body, chunk, blocks, part, len(before)),
        grid_spec=pltpu.PrefetchScalarGridSpec(
            num_scalar_prefetch=3,
            grid=(2, groups, few),
            in_specs=[q_spec, kv_spec, kv_spec, o_spec, o_spec, lse_spec] + [kv_spec] * len(before),
            out_specs=[o_spec, kv_spec, kv_spec],
            scratch_shapes=[
                pltpu.VMEM((ys * half, HD), bf16),
                pltpu.VMEM((ys * half, HD), bf16),
                pltpu.VMEM((REP * HD, chunk), f32),
                pltpu.VMEM((ys, HD, half), f32),
                pltpu.VMEM((ys, HD, half), f32),
                pltpu.VMEM((8, chunk), f32),
            ],
        ),
        out_shape=[
            jax.ShapeDtypeStruct((queries.shape[0], half), f32),
            jax.ShapeDtypeStruct(keys.shape, kind),
            jax.ShapeDtypeStruct(keys.shape, kind),
        ],
        compiler_params=pltpu.CompilerParams(vmem_limit_bytes=VMEM_BYTES),
        cost_estimate=estimate(
            pairs * REP * chunk * chunk * HD * 10 * 4,
            queries.size * 6 + keys.size * 16,
            pairs * REP * chunk * chunk,
        ),
        name="attention_backward",
    )(qpos, kpos, lengths, queries, keys, values, attended, grads, lse, *before)


def rotate(vectors, cos_table, sin_table, back=False):
    heads = vectors.shape[0] // HD
    halves = vectors.reshape(heads, 2, HD // 2, vectors.shape[1])
    a, b = halves[:, 0], halves[:, 1]
    sin_table = -sin_table if back else sin_table
    turned = jnp.stack([a * cos_table - b * sin_table, b * cos_table + a * sin_table], axis=1)
    return turned.reshape(vectors.shape)


def contract(left, right, left_dim, right_dim):
    return lax.dot_general(
        left, right, (((left_dim,), (right_dim,)), ((), ())), preferred_element_type=f32
    )


def body(
    tokens_in, grad_out, seq_lengths, stretch_order, attn_gain, query_w, key_w, value_w,
    output_w, mlp_gain, gate_w, up_w, down_w,
):
    zs, ys = lax.axis_size("z"), lax.axis_size("y")
    z, c, y, x = (lax.axis_index(name) for name in ("z", "c", "y", "x"))
    rows, width = tokens_in.shape[1:]
    chunk = rows // 2
    unit = width // (zs * ys)

    def to_slots(value):
        if (unit // 2) % 128 == 0:
            return move_columns(value, y[None], zs, ys, True)
        parts = value.reshape(value.shape[0], zs, 2, ys, unit // 2)
        parts = [lax.dynamic_index_in_dim(parts, (y - k) % ys, 3) for k in range(ys)]
        return jnp.concatenate(
            [jnp.transpose(p, (0, 3, 1, 2, 4)).reshape(value.shape[0], width // ys) for p in parts],
            axis=1,
        )

    def from_slots(value):
        if (unit // 2) % 128 == 0:
            return move_columns(value, y[None], zs, ys, False)
        parts = value.reshape(value.shape[0], ys, zs, 2, unit // 2)
        parts = jnp.stack(
            [lax.dynamic_index_in_dim(parts, (y - k) % ys, 1, keepdims=False) for k in range(ys)], axis=3
        )
        return parts.reshape(value.shape[0], width)

    orders = jnp.stack([stretch_order[0], shift(stretch_order[0], "c", 1)])
    lengths = jnp.concatenate([seq_lengths, shift(seq_lengths, "c", 1)])
    slots = [
        2 * (((y - k) % ys) * 2 + (x if i == 0 else 1 - x)) + b
        for k in range(ys)
        for i in range(2)
        for b in range(2)
    ]
    kpos = jnp.stack([lax.dynamic_index_in_dim(orders, s, 1, keepdims=False) for s in slots], axis=1)
    qpos = kpos[:, :4]
    token_pos = (qpos[:, :, None] * chunk + jnp.arange(chunk, dtype=jnp.int32)).reshape(4 * rows)
    own_pos = token_pos[:rows]
    live = (own_pos < seq_lengths[0]).astype(f32)[:, None]
    angles = frequencies()[:, None] * token_pos.astype(f32)[None, :]
    cos_table, sin_table = jnp.cos(angles), jnp.sin(angles)

    gains = jnp.stack([attn_gain, mlp_gain])
    gains = in_order(gains, shift(gains, "x", 1), x, 1)
    gains = in_order(gains, shift(gains, "c", 1), c, 1)
    gains = gather_gains(gains).astype(f32)
    gain_one, gain_two = gains[0:1], gains[1:2]

    inputs = to_slots(tokens_in[0]).astype(f32)
    scale_one = lax.rsqrt(jnp.mean(inputs * inputs, axis=1, keepdims=True) + epsilon)
    unit_one = inputs * scale_one
    normed_own = (unit_one * gain_one).astype(bf16)

    def packed(*weights):
        return jnp.concatenate(
            [w[:, t * (w.shape[1] // 4) : (t + 1) * (w.shape[1] // 4)] for t in range(4) for w in weights],
            axis=1,
        )

    nq, nk = query_w.shape[1] // 4, key_w.shape[1] // 4
    nqkv = nq + 2 * nk
    attn_unit = spread_columns(packed(query_w, key_w, value_w, output_w), c, x)
    qkv_unit, out_unit = attn_unit[:, :nqkv], attn_unit[:, nqkv:]
    mlp_unit = spread_columns(packed(gate_w, up_w, down_w), c, x, (attn_unit,), (normed_own,))
    nf = gate_w.shape[1] // 4
    gate_unit, up_unit, down_unit = (mlp_unit[:, i * nf : (i + 1) * nf] for i in range(3))
    qkv_slots = gather_slots(gather_column(qkv_unit))
    own, beside, sibling, both_two = group_tokens(normed_own)
    out_column = hold(gather_column(hold(out_unit, normed_own)), beside)
    qkv_w = jnp.concatenate(qkv_slots, axis=0)
    out_slots = gather_slots(out_column)
    out_w = jnp.concatenate(out_slots, axis=0)
    gate_column = gather_column(hold(gate_unit, out_column))
    up_all, down_all = gather_whole(up_unit, y), gather_whole(down_unit, y)

    normed_one = jnp.concatenate([own, beside, sibling, both_two], axis=0)
    pre = contract(after(qkv_w, mlp_unit), normed_one, 0, 1)
    queries = (rotate(pre[:nq], cos_table, sin_table).astype(bf16)) * jnp.asarray(0.125, bf16)
    key_own = rotate(pre[nq : nq + nk], cos_table, sin_table).astype(bf16)
    value_own = pre[nq + nk :].astype(bf16)
    both_own = jnp.concatenate([key_own, value_own], axis=0)
    both = jnp.stack([both_own] + [shift(both_own, "y", k) for k in range(1, ys)])
    keys, values = both[:, :nk], both[:, nk:]
    gate_column = hold(gate_column, both)
    cut = gate_column.shape[0] // 2
    gate_first = [shift(gate_column[:cut], "y", k) for k in range(1, ys)]
    gate_rest = [shift(gate_column[cut:], "y", k) for k in range(1, ys)]
    grad_own = to_slots(grad_out[0]) * live.astype(bf16)
    grad_rows = grad_own.astype(f32)
    own, beside, sibling, both_two = group_tokens(hold(grad_own, both_own))
    grad_low = jnp.concatenate([own, sibling, both_two, beside], axis=0)

    attended_one, lse_one = attention_fwd(
        after(queries, grad_own, out_w), keys, values, qpos, kpos, lengths, chunk, 1
    )
    branch = contract(attended_one, out_w, 0, 1).astype(bf16)
    from_sibling = shift(branch[:rows], "c", 1)
    beside_sum = branch[rows:].astype(f32) + from_sibling.astype(f32)
    from_beside = shift(beside_sum.astype(bf16), "x", 1)
    attended_zero, lse_zero = attention_fwd(
        after(queries, from_sibling, both_two), keys, values, qpos, kpos, lengths, chunk, 0
    )
    branch = contract(after(attended_zero, from_beside, *gate_first), out_w, 0, 1).astype(bf16)
    middle = inputs + branch[:rows].astype(f32) + shift(branch[rows:], "c", 1).astype(f32) + from_beside.astype(f32)
    gate_all = [gate_column] + [jnp.concatenate(two, axis=0) for two in zip(gate_first, gate_rest)]
    attended = jnp.concatenate([attended_zero, attended_one], axis=1)
    scale_two = lax.rsqrt(jnp.mean(middle * middle, axis=1, keepdims=True) + epsilon)
    unit_two = middle * scale_two
    own, beside, sibling, both_two = group_tokens((unit_two * gain_two).astype(bf16))
    normed_two = jnp.concatenate([own, sibling, both_two, after(beside, *gate_rest)], axis=0)

    (gate_pre,) = rows_product(normed_two, gate_all, [], plain, 1, "gate")
    up_pre, hidden = rows_product(normed_two, up_all, [gate_pre], up_finish, 2, "up")

    def finish(total):
        return join_columns(total, c, x)

    by_y = (y - jnp.arange(ys, dtype=jnp.int32)) % ys
    last = columns_product(grad_low, by_y, ys, hidden, [], "down_grad")
    down_grad = scatter_whole(last)
    grad_gate, grad_up = rows_product(
        after(grad_low, last), down_all, [gate_pre, up_pre], hidden_back, 2, "hidden_grad"
    )
    norm_parts, last = [], grad_gate
    for g, u in zip(gate_all, up_all):
        last = turned_product([after(grad_gate, last), grad_up], [g, u], "norm_grad")
        norm_parts.append(last)
    sums = [scatter_by_c(part, False) for part in norm_parts]
    came = [shift(beside.astype(bf16), "x", 1) for _, beside in sums]
    last = columns_product(after(normed_two, last), by_y, ys, grad_gate, [], "gate_grad")
    gate_grad = scatter_whole(last)
    came[0] = after(came[0], last)
    last = columns_product(after(normed_two, last), by_y, ys, grad_up, [], "up_grad")
    up_grad = scatter_whole(last)
    came[-1] = after(came[-1], last)
    grad_norm_two = jnp.concatenate([mine + got.astype(f32) for (mine, _), got in zip(sums, came)], axis=1)
    gain_two_grad = jnp.sum(grad_norm_two * unit_two, axis=0)
    def gain_back(terms):
        own, other = halves(scatter_gains(terms, unit), c, 0)
        own, other = halves(own + shift(other, "c", 1), x, 0)
        return own + shift(other, "x", 1)

    scaled_two = grad_norm_two * gain_two
    grad_middle = grad_rows + scale_two * (
        scaled_two - unit_two * jnp.mean(scaled_two * unit_two, axis=1, keepdims=True)
    )

    def attn_terms(activations, grads, k):
        size = width // ys
        return contract(lax.dynamic_slice_in_dim(activations, k * size, size, 1), grads, 0, 1)

    own = grad_middle.astype(bf16)
    beside, sibling = shift(own, "x", 1), shift(own, "c", 1)
    grad_attn = contract(out_w, jnp.concatenate([own, sibling], axis=0), 0, 1).astype(bf16)
    query_zero, grad_keys, grad_values = attention_bwd(
        after(queries, down_grad), keys, values, attended_zero, grad_attn, lse_zero, qpos, kpos, lengths,
        chunk, 0,
    )
    beside = hold(beside, query_zero)
    both_two = shift(beside, "c", 1)
    branch_parts, last = [], query_zero
    for w in down_all:
        last = turned_product([after(hidden, last)], [w], "down")
        branch_parts.append(last)
    sent = [part[rows : 3 * rows] for part in branch_parts]
    got_c = [shift(part, "c", 1) for part in sent]
    down_own, down_got = join_by_c(hold(down_grad, query_zero), c)
    grad_attn = contract(out_w, jnp.concatenate([both_two, after(beside, last)], axis=0), 0, 1).astype(bf16)
    query_one, grad_keys, grad_values = attention_bwd(
        after(queries, gate_grad, down_got, *got_c), keys, values, attended_one, grad_attn, lse_one, qpos,
        kpos, lengths, chunk, 1, grad_keys, grad_values,
    )
    got_x = [
        shift((part[3 * rows :].astype(f32) + got[rows:].astype(f32)).astype(bf16), "x", 1)
        for part, got in zip(branch_parts, got_c)
    ]
    down_own, down_got = join_by_x(down_own, down_got, c, x)
    query_one = after(query_one, down_got, *got_x)
    down_grad = in_order(down_own, down_got, x, 1)
    branch_two = jnp.concatenate(
        [
            part[:rows].astype(f32) + from_c[:rows].astype(f32) + from_x.astype(f32)
            for part, from_c, from_x in zip(branch_parts, got_c, got_x)
        ],
        axis=1,
    )
    result = from_slots(((middle + branch_two) * live).astype(bf16))[None]
    grad_branch = jnp.concatenate([own, sibling, both_two, beside], axis=0)
    grad_branch = jnp.concatenate([own, sibling, both_two, beside], axis=0)
    gain_two_back = gain_back(hold(gain_two_grad, query_one))
    def pick(table, *chunks):
        return jnp.concatenate([table[:, i * rows : (i + 1) * rows] for i in chunks], axis=1)

    grad_both = jnp.concatenate([grad_keys, grad_values], axis=1)
    got = [shift(grad_both[k], "y", -k) for k in range(1, ys)]
    grad_both = sum([grad_both[0].astype(f32)] + [term.astype(f32) for term in got])
    turned_zero = rotate(query_zero, pick(cos_table, 0, 2), pick(sin_table, 0, 2), True).astype(bf16)
    turned_one = rotate(query_one, pick(cos_table, 3, 1), pick(sin_table, 3, 1), True).astype(bf16)
    grad_query = jnp.concatenate(
        [turned_zero[:, :rows], turned_one[:, rows:], turned_zero[:, rows:], turned_one[:, :rows]], axis=1
    )
    grad_qkv = jnp.concatenate(
        [
            grad_query,
            rotate(grad_both[:nk], cos_table, sin_table, True).astype(bf16),
            grad_both[nk:].astype(bf16),
        ],
        axis=0,
    )
    qkv_sent = send_slots([attn_terms(normed_one, grad_qkv, k).astype(bf16) for k in range(1, ys)])
    partial = contract(grad_qkv, qkv_w, 0, 1).astype(bf16)
    mine, beside_sum = scatter_by_c(partial, True)
    from_beside = shift(beside_sum.astype(bf16), "x", 1)
    output_grad = scatter_whole(
        jnp.concatenate(
            [attn_terms(hold(grad_branch, from_beside), attended, by_y[i]) for i in range(ys)], axis=0
        ).astype(bf16)
    )
    gate_grad = finish(hold(gate_grad, from_beside))
    grad_norm_one = mine + from_beside.astype(f32)
    qkv_grad = sum([attn_terms(normed_one, grad_qkv, 0)] + [t.astype(f32) for t in qkv_sent])
    qkv_grad = scatter_column(hold(qkv_grad.astype(bf16), up_grad))
    gain_one_grad = jnp.sum(grad_norm_one * unit_one, axis=0)
    scaled_one = grad_norm_one * gain_one
    up_grad = finish(hold(up_grad, from_beside))
    grad_inputs = grad_middle + scale_one * (
        scaled_one - unit_one * jnp.mean(scaled_one * unit_one, axis=1, keepdims=True)
    )

    qkv_back = finish(qkv_grad)

    def columns(low, high):
        return jnp.concatenate(
            [qkv_back[:, t * nqkv + low : t * nqkv + high] for t in range(4)], axis=1
        ).astype(f32)

    return (
        result,
        from_slots(grad_inputs)[None],
        gain_back(gain_one_grad),
        columns(0, nq),
        columns(nq, nq + nk),
        columns(nq + nk, nqkv),
        finish(output_grad).astype(f32),
        gain_two_back,
        gate_grad.astype(f32),
        up_grad.astype(f32),
        down_grad.astype(f32),
    )


def solution(mesh):
    dp, seq = mesh.shape["dp"], mesh.shape["seq"]
    fine = Mesh(mesh.devices.reshape(dp // 2, 2, seq // 2, 2), ("z", "c", "y", "x"))
    every = ("z", "c", "y", "x")
    tokens = P(("z", "c"), ("y", "x"), None)
    vector, matrix = P(every), P(every, None)
    return jax.shard_map(
        body,
        mesh=fine,
        in_specs=(
            tokens, tokens, P(("z", "c")), P(("z", "c"), None), vector, matrix, matrix, matrix,
            matrix, vector, matrix, matrix, matrix,
        ),
        out_specs=(
            tokens, tokens, vector, matrix, matrix, matrix, matrix, vector, matrix, matrix, matrix,
        ),
        check_vma=False,
    )
```

```python
import functools
import math

import jax
import jax.numpy as jnp
from jax import lax
from jax.experimental import pallas as pl
from jax.experimental.pallas import tpu as pltpu
from jax.sharding import Mesh
from jax.sharding import PartitionSpec as P

HEADS = 32
KVH = 8
HD = 64
REP = HEADS // KVH

epsilon = 1e-05
masked_score = -1e30
floor_score = -1e29

bf16 = jnp.bfloat16
f32 = jnp.float32


def frequencies():
    steps_even = jnp.arange(0, HD, 2).astype(f32) / HD
    base_freq = 1.0 / 500000.0**steps_even
    wavelength = 2.0 * math.pi / base_freq
    smooth = (8192.0 / wavelength - 1.0) / 3.0
    blended = (1.0 - smooth) * base_freq / 32.0 + smooth * base_freq
    return jnp.where(
        wavelength < 2048.0, base_freq, jnp.where(wavelength > 8192.0, base_freq / 32.0, blended)
    )


def shift(value, axis, steps):
    size = lax.axis_size(axis)
    return lax.ppermute(value, axis, [(i, (i + steps) % size) for i in range(size)])


def in_order(own, other, index, axis):
    return jnp.where(
        index == 0,
        jnp.concatenate([own, other], axis=axis),
        jnp.concatenate([other, own], axis=axis),
    )


def halves(value, index, axis):
    size = value.shape[axis] // 2
    return (
        lax.dynamic_slice_in_dim(value, index * size, size, axis),
        lax.dynamic_slice_in_dim(value, (1 - index) * size, size, axis),
    )


def spread_columns(shard, c, x, earlier=(), later=()):
    own, other = halves(shard, x, 1)
    if earlier:
        other = hold(other, *earlier)
    both = in_order(own, after(shift(other, "x", 1), *later), x, 0)
    own, other = halves(both, c, 1)
    return in_order(own, shift(other, "c", 1), c, 0)


def join_by_c(unit, c):
    own, other = halves(unit, c, 0)
    return own, shift(other, "c", 1)


def join_by_x(own, got, c, x):
    own, other = halves(in_order(own, got, c, 1), x, 0)
    return own, shift(other, "x", 1)


def join_columns(unit, c, x):
    own, got = join_by_x(*join_by_c(unit, c), c, x)
    return in_order(own, got, x, 1)


def after(value, *others):
    return lax.optimization_barrier((value,) + others)[0]


def hold_body(*refs):
    del refs


def hold(value, *others):
    return pl.pallas_call(
        hold_body,
        in_specs=[pl.BlockSpec(memory_space=pl.ANY)] * (1 + len(others)),
        out_specs=pl.BlockSpec(memory_space=pl.ANY),
        out_shape=jax.ShapeDtypeStruct(value.shape, value.dtype),
        input_output_aliases={0: 0},
        name="hold",
    )(value, *others)


def gather_column(unit):
    return lax.all_gather(unit, "z", axis=0, tiled=True)


def gather_slots(column):
    return [column] + [shift(column, "y", k) for k in range(1, lax.axis_size("y"))]


def send_slots(terms):
    return [shift(term, "y", -(k + 1)) for k, term in enumerate(terms)]


def gather_whole(unit, y):
    zs, ys = lax.axis_size("z"), lax.axis_size("y")
    size = zs * unit.shape[0]
    whole = lax.all_gather(unit, ("y", "z"), axis=0, tiled=True)
    return [lax.dynamic_slice_in_dim(whole, ((y - k) % ys) * size, size, 0) for k in range(ys)]


def scatter_whole(terms):
    return lax.psum_scatter(terms, ("y", "z"), scatter_dimension=0, tiled=True)


def scatter_column(total):
    return lax.psum_scatter(total, "z", scatter_dimension=0, tiled=True)


def gather_gains(unit):
    zs, ys = lax.axis_size("z"), lax.axis_size("y")
    row = jnp.stack([unit] + [shift(unit, "y", k) for k in range(1, ys)], axis=1)
    z = lax.axis_index("z")
    out = jnp.zeros((2, ys, zs, unit.shape[1]), unit.dtype)
    for j in range(zs):
        got = row if j == 0 else shift(row, "z", j)
        out = lax.dynamic_update_slice(out, got[:, :, None], (0, 0, (z - j) % zs, 0))
    return out.reshape(2, -1)


def scatter_gains(terms, unit):
    zs, ys = lax.axis_size("z"), lax.axis_size("y")
    z = lax.axis_index("z")
    terms = terms.reshape(ys, zs * unit)
    total = terms[0]
    for k in range(1, ys):
        total = total + shift(terms[k], "y", -k)
    total = total.reshape(zs, unit)
    out = lax.dynamic_index_in_dim(total, z, 0, keepdims=False)
    for j in range(1, zs):
        out = out + shift(lax.dynamic_index_in_dim(total, (z - j) % zs, 0, keepdims=False), "z", -j)
    return out


def group_tokens(own):
    beside = shift(own, "x", 1)
    return own, beside, shift(own, "c", 1), shift(beside, "c", 1)


def scatter_by_c(partial, by_sequence):
    count = partial.shape[0] // 4
    mine = partial[:count]
    if by_sequence:
        beside, sent = partial[count : 2 * count], partial[2 * count :]
    else:
        beside, sent = partial[3 * count :], partial[count : 3 * count]
    got = shift(sent, "c", 1).astype(f32)
    return mine.astype(f32) + got[:count], beside.astype(f32) + got[count:]


def scatter_tokens(partials, by_sequence):
    sums = []
    for partial in partials:
        mine, beside = scatter_by_c(partial, by_sequence)
        sums.append(mine + shift(beside.astype(bf16), "x", 1).astype(f32))
    return jnp.concatenate(sums, axis=1)


def move_columns_body(zs, ys, forth, y_ref, in_ref, out_ref):
    block = in_ref.shape[1] // (zs * 2 * ys)
    y = y_ref[0]
    for i in range(zs * 2):
        for k in range(ys):
            natural = i * ys + lax.rem(y - k + ys, ys)
            natural = pl.ds(pl.multiple_of(natural * block, block), block)
            slot = pl.ds((k * zs * 2 + i) * block, block)
            if forth:
                out_ref[:, slot] = in_ref[:, natural]
            else:
                out_ref[:, natural] = in_ref[:, slot]


def move_columns(value, y, zs, ys, forth):
    rows, width = value.shape
    tall = rows // 4
    spec = pl.BlockSpec((tall, width), lambda i, *_: (i, 0))
    return pl.pallas_call(
        functools.partial(move_columns_body, zs, ys, forth),
        grid_spec=pltpu.PrefetchScalarGridSpec(
            num_scalar_prefetch=1, grid=(4,), in_specs=[spec], out_specs=spec
        ),
        out_shape=jax.ShapeDtypeStruct(value.shape, value.dtype),
        cost_estimate=pl.CostEstimate(
            flops=0, bytes_accessed=2 * value.size * value.dtype.itemsize, transcendentals=0
        ),
        name="move_columns",
    )(y, value)


VMEM_BYTES = 56 * 1024 * 1024
EASE = 1


def estimate(flops, moved, exps=0):
    return pl.CostEstimate(
        flops=int(flops) // EASE, bytes_accessed=int(moved) // EASE, transcendentals=int(exps) // EASE
    )


def fit(size, most):
    return size if size <= most else fit(size // 2, most)


def rows_product(left, parts, extras, finish, n_out, name):
    t, d = left.shape
    n = parts[0].shape[1]
    depth = parts[0].shape[0]
    bm, bn = fit(t, 512), fit(n, 1024)
    n_parts, n_extra = len(parts), len(extras)

    def kernel(*refs):
        left_ref = refs[0]
        product = None
        for p in range(n_parts):
            term = jnp.dot(
                left_ref[:, p * depth : (p + 1) * depth], refs[1 + p][...], preferred_element_type=f32
            )
            product = term if product is None else product + term
        got = finish(product, *(r[...] for r in refs[1 + n_parts : 1 + n_parts + n_extra]))
        for ref, value in zip(refs[1 + n_parts + n_extra :], got):
            ref[...] = value.astype(bf16)

    tile = pl.BlockSpec((bm, bn), lambda j, i: (i, j))
    return pl.pallas_call(
        kernel,
        grid=(n // bn, t // bm),
        in_specs=[pl.BlockSpec((bm, d), lambda j, i: (i, 0))]
        + [pl.BlockSpec((depth, bn), lambda j, i: (0, j))] * n_parts
        + [tile] * n_extra,
        out_specs=[tile] * n_out,
        out_shape=[jax.ShapeDtypeStruct((t, n), bf16)] * n_out,
        compiler_params=pltpu.CompilerParams(vmem_limit_bytes=VMEM_BYTES),
        cost_estimate=estimate(2 * t * d * n, 2 * (t * d + d * n + t * n)),
        name=name,
    )(left, *parts, *extras)


def turned_product(lefts, rights, name):
    t, f = lefts[0].shape
    n = rights[0].shape[0]
    bm, bn = fit(t, 512), fit(n, 1024)
    count = len(lefts)

    def kernel(*refs):
        product = None
        for p in range(count):
            term = lax.dot_general(
                refs[p][...], refs[count + p][...], (((1,), (1,)), ((), ())), preferred_element_type=f32
            )
            product = term if product is None else product + term
        refs[2 * count][...] = product.astype(bf16)

    return pl.pallas_call(
        kernel,
        grid=(n // bn, t // bm),
        in_specs=[pl.BlockSpec((bm, f), lambda j, i: (i, 0))] * count
        + [pl.BlockSpec((bn, f), lambda j, i: (j, 0))] * count,
        out_specs=pl.BlockSpec((bm, bn), lambda j, i: (i, j)),
        out_shape=jax.ShapeDtypeStruct((t, n), bf16),
        compiler_params=pltpu.CompilerParams(vmem_limit_bytes=VMEM_BYTES),
        cost_estimate=estimate(2 * count * t * f * n, 2 * count * (t * f + f * n)),
        name=name,
    )(*lefts, *rights)


def columns_product(left, slots, n_parts, right, others, name):
    t, d = left.shape
    m = d // n_parts
    f = right.shape[1]
    bm, bn = fit(m, 512), fit(f, 1024)
    per = m // bm
    count = len(others)

    def kernel(slots_ref, left_ref, right_ref, *refs):
        turned_ref = refs[-1]

        @pl.when(pl.program_id(1) == 0)
        def _():
            turned_ref[...] = left_ref[...].T

        product = jnp.dot(turned_ref[...], right_ref[...], preferred_element_type=f32)
        for ref in refs[:count]:
            product = product + ref[...].astype(f32)
        refs[count][...] = product.astype(bf16)

    rows = slots.shape[0] * m
    tile = pl.BlockSpec((bm, bn), lambda i, j, slots_ref: (i, j))
    return pl.pallas_call(
        kernel,
        grid_spec=pltpu.PrefetchScalarGridSpec(
            num_scalar_prefetch=1,
            grid=(rows // bm, f // bn),
            in_specs=[
                pl.BlockSpec((t, bm), lambda i, j, slots_ref: (0, slots_ref[i // per] * per + i % per)),
                pl.BlockSpec((t, bn), lambda i, j, slots_ref: (0, j)),
            ]
            + [tile] * count,
            out_specs=tile,
            scratch_shapes=[pltpu.VMEM((bm, t), bf16)],
        ),
        out_shape=jax.ShapeDtypeStruct((rows, f), bf16),
        compiler_params=pltpu.CompilerParams(vmem_limit_bytes=VMEM_BYTES),
        cost_estimate=estimate(2 * t * rows * f, 2 * (t * m + t * f + rows * f)),
        name=name,
    )(slots, left, right, *others)


def plain(product):
    return (product,)


def up_finish(product, gate):
    gate = gate.astype(f32)
    return product, gate * jax.nn.sigmoid(gate) * product


def hidden_back(grad, gate, up):
    gate, up = gate.astype(f32), up.astype(f32)
    sigmoid = jax.nn.sigmoid(gate)
    return grad * up * sigmoid * (1.0 + gate * (1.0 - sigmoid)), grad * gate * sigmoid


def seen(chunk, first, qp, length):
    shape = (chunk, REP * chunk)
    at_key = first + lax.broadcasted_iota(jnp.int32, shape, 0)
    at_query = qp * chunk + (lax.broadcasted_iota(jnp.int32, shape, 1) & (chunk - 1))
    return (at_key <= at_query) & (at_key < length)


def attention_fwd_body(
    chunk, blocks, part, qpos_ref, kpos_ref, len_ref, q_ref, k_ref, v_ref, o_ref, lse_ref,
    kn_ref, q4_ref, m_ref, l_ref, acc_ref,
):
    s, qb = pl.program_id(0), pl.program_id(2)
    ys = k_ref.shape[0]

    @pl.when(qb == 0)
    def _():
        for yk in range(ys):
            for b in range(blocks):
                kn_ref[pl.ds((yk * blocks + b) * chunk, chunk), :] = (
                    k_ref[yk, :, pl.ds(b * chunk, chunk)].astype(f32).T.astype(bf16)
                )

    qp = qpos_ref[s, part * (blocks // 2) + qb]
    length = len_ref[s]
    for h in range(REP):
        q4_ref[:, h * chunk : (h + 1) * chunk] = q_ref[h * HD : (h + 1) * HD, :]
    m_ref[...] = jnp.full_like(m_ref, floor_score)
    l_ref[...] = jnp.zeros_like(l_ref)
    acc_ref[...] = jnp.zeros_like(acc_ref)

    for yk in range(ys):

        def step(b, carry, yk=yk):
            kp = kpos_ref[s, yk * blocks + b]
            first = kp * chunk
            live = (kp <= qp) & (first < length)
            partly = (kp == qp) | (first + chunk > length)

            def work(masked):
                kn = kn_ref[pl.ds(pl.multiple_of((yk * blocks + b) * chunk, chunk), chunk), :]
                vt = v_ref[yk, :, pl.ds(pl.multiple_of(b * chunk, chunk), chunk)]
                scores = jnp.dot(kn, q4_ref[...], preferred_element_type=f32)
                if masked:
                    scores = jnp.where(seen(chunk, first, qp, length), scores, masked_score)
                m_old = m_ref[...]
                m_new = jnp.maximum(m_old, jnp.max(scores, axis=0, keepdims=True))
                alpha = jnp.exp(m_old - m_new)
                probs = jnp.exp(scores - m_new)
                m_ref[...] = m_new
                l_ref[...] = l_ref[...] * alpha + jnp.sum(probs, axis=0, keepdims=True)
                acc_ref[...] = acc_ref[...] * alpha + jnp.dot(
                    vt, probs.astype(bf16), preferred_element_type=f32
                )

            pl.when(live & partly)(lambda: work(True))
            pl.when(live & jnp.logical_not(partly))(lambda: work(False))
            return carry

        lax.fori_loop(0, blocks, step, 0)

    out = (acc_ref[...] / l_ref[...]).astype(bf16)
    lse = m_ref[...] + jnp.log(l_ref[...])
    for h in range(REP):
        columns = slice(h * chunk, (h + 1) * chunk)
        o_ref[h * HD : (h + 1) * HD, :] = out[:, columns]
        lse_ref[0, h : h + 1, :] = lse[:, columns]


def attention_fwd(queries, keys, values, qpos, kpos, lengths, chunk, part):
    tokens = queries.shape[1]
    groups = queries.shape[0] // (REP * HD)
    ys = keys.shape[0]
    half = tokens // 2
    blocks = half // chunk
    few = blocks // 2
    q_spec = pl.BlockSpec((REP * HD, chunk), lambda s, g, b, *_: (g, s * blocks + part * few + b))
    o_spec = pl.BlockSpec((REP * HD, chunk), lambda s, g, b, *_: (g, ((s + part) % 2) * few + b))
    kv_spec = pl.BlockSpec((ys, HD, half), lambda s, g, b, *_: (0, g, s))
    lse_spec = pl.BlockSpec((1, REP, chunk), lambda s, g, b, *_: (g, 0, ((s + part) % 2) * few + b))
    pairs = 2 * groups * few * blocks * ys
    return pl.pallas_call(
        functools.partial(attention_fwd_body, chunk, blocks, part),
        grid_spec=pltpu.PrefetchScalarGridSpec(
            num_scalar_prefetch=3,
            grid=(2, groups, few),
            in_specs=[q_spec, kv_spec, kv_spec],
            out_specs=[o_spec, lse_spec],
            scratch_shapes=[
                pltpu.VMEM((ys * half, HD), bf16),
                pltpu.VMEM((HD, REP * chunk), bf16),
                pltpu.VMEM((1, REP * chunk), f32),
                pltpu.VMEM((1, REP * chunk), f32),
                pltpu.VMEM((HD, REP * chunk), f32),
            ],
        ),
        compiler_params=pltpu.CompilerParams(vmem_limit_bytes=VMEM_BYTES),
        out_shape=[
            jax.ShapeDtypeStruct((queries.shape[0], half), bf16),
            jax.ShapeDtypeStruct((groups, REP, half), f32),
        ],
        cost_estimate=estimate(
            pairs * REP * chunk * chunk * HD * 4 * 8,
            queries.size * 2 + keys.size * 4,
            pairs * REP * chunk * chunk,
        ),
        name="attention_forward",
    )(qpos, kpos, lengths, queries, keys, values)


def attention_bwd_body(
    chunk, blocks, part, n_before, qpos_ref, kpos_ref, len_ref, q_ref, k_ref, v_ref, o_ref, do_ref,
    lse_ref, *refs,
):
    before = refs[:n_before]
    dq_ref, dk_ref, dv_ref, kn_ref, vn_ref, q4_ref, do4_ref, dqa_ref, dka_ref, dva_ref, row_ref = refs[n_before:]
    s, qb = pl.program_id(0), pl.program_id(2)
    ys = k_ref.shape[0]

    @pl.when(qb == 0)
    def _():
        if before:
            dka_ref[...] = before[0][...]
            dva_ref[...] = before[1][...]
        else:
            dka_ref[...] = jnp.zeros_like(dka_ref)
            dva_ref[...] = jnp.zeros_like(dva_ref)
        for yk in range(ys):
            for b in range(blocks):
                rows = pl.ds((yk * blocks + b) * chunk, chunk)
                cols = pl.ds(b * chunk, chunk)
                kn_ref[rows, :] = k_ref[yk, :, cols].astype(f32).T.astype(bf16)
                vn_ref[rows, :] = v_ref[yk, :, cols].astype(f32).T.astype(bf16)

    qp = qpos_ref[s, part * (blocks // 2) + qb]
    length = len_ref[s]
    dqa_ref[...] = jnp.zeros_like(dqa_ref)
    for h in range(REP):
        rows, columns = slice(h * HD, (h + 1) * HD), slice(h * chunk, (h + 1) * chunk)
        q4_ref[:, columns] = q_ref[rows, :]
        do4_ref[:, columns] = do_ref[rows, :]
        row_ref[0:1, columns] = lse_ref[0, h : h + 1, :]
        row_ref[1:2, columns] = jnp.sum(
            do_ref[rows, :].astype(f32) * o_ref[rows, :].astype(f32), axis=0, keepdims=True
        )

    for yk in range(ys):

        def step(b, carry, yk=yk):
            kp = kpos_ref[s, yk * blocks + b]
            first = kp * chunk
            live = (kp <= qp) & (first < length)
            partly = (kp == qp) | (first + chunk > length)

            def work(masked):
                at = pl.ds(pl.multiple_of((yk * blocks + b) * chunk, chunk), chunk)
                cols = pl.ds(pl.multiple_of(b * chunk, chunk), chunk)
                q4, do4 = q4_ref[...], do4_ref[...]
                scores = jnp.dot(kn_ref[at, :], q4, preferred_element_type=f32)
                if masked:
                    scores = jnp.where(seen(chunk, first, qp, length), scores, masked_score)
                probs = jnp.exp(scores - row_ref[0:1, :])
                grad_probs = jnp.dot(vn_ref[at, :], do4, preferred_element_type=f32)
                grad_scores = (probs * (grad_probs - row_ref[1:2, :])).astype(bf16)
                across = (((1,), (1,)), ((), ()))
                dva_ref[yk, :, cols] += lax.dot_general(
                    do4, probs.astype(bf16), across, preferred_element_type=f32
                )
                dqa_ref[...] += jnp.dot(k_ref[yk, :, cols], grad_scores, preferred_element_type=f32)
                dka_ref[yk, :, cols] += lax.dot_general(
                    q4, grad_scores, across, preferred_element_type=f32
                )

            pl.when(live & partly)(lambda: work(True))
            pl.when(live & jnp.logical_not(partly))(lambda: work(False))
            return carry

        lax.fori_loop(0, blocks, step, 0)

    for h in range(REP):
        dq_ref[h * HD : (h + 1) * HD, :] = dqa_ref[:, h * chunk : (h + 1) * chunk] * 0.125

    @pl.when(qb == blocks // 2 - 1)
    def _():
        dk_ref[...] = dka_ref[...].astype(dk_ref.dtype)
        dv_ref[...] = dva_ref[...].astype(dv_ref.dtype)


def attention_bwd(queries, keys, values, attended, grads, lse, qpos, kpos, lengths, chunk, part, *before):
    tokens = queries.shape[1]
    groups = queries.shape[0] // (REP * HD)
    ys = keys.shape[0]
    half = tokens // 2
    blocks = half // chunk
    few = blocks // 2
    q_spec = pl.BlockSpec((REP * HD, chunk), lambda s, g, b, *_: (g, s * blocks + part * few + b))
    o_spec = pl.BlockSpec((REP * HD, chunk), lambda s, g, b, *_: (g, ((s + part) % 2) * few + b))
    kv_spec = pl.BlockSpec((ys, HD, half), lambda s, g, b, *_: (0, g, s))
    lse_spec = pl.BlockSpec((1, REP, chunk), lambda s, g, b, *_: (g, 0, ((s + part) % 2) * few + b))
    pairs = 2 * groups * few * blocks * ys
    kind = bf16 if before else f32
    return pl.pallas_call(
        functools.partial(attention_bwd_body, chunk, blocks, part, len(before)),
        grid_spec=pltpu.PrefetchScalarGridSpec(
            num_scalar_prefetch=3,
            grid=(2, groups, few),
            in_specs=[q_spec, kv_spec, kv_spec, o_spec, o_spec, lse_spec] + [kv_spec] * len(before),
            out_specs=[o_spec, kv_spec, kv_spec],
            scratch_shapes=[
                pltpu.VMEM((ys * half, HD), bf16),
                pltpu.VMEM((ys * half, HD), bf16),
                pltpu.VMEM((HD, REP * chunk), bf16),
                pltpu.VMEM((HD, REP * chunk), bf16),
                pltpu.VMEM((HD, REP * chunk), f32),
                pltpu.VMEM((ys, HD, half), f32),
                pltpu.VMEM((ys, HD, half), f32),
                pltpu.VMEM((2, REP * chunk), f32),
            ],
        ),
        out_shape=[
            jax.ShapeDtypeStruct((queries.shape[0], half), f32),
            jax.ShapeDtypeStruct(keys.shape, kind),
            jax.ShapeDtypeStruct(keys.shape, kind),
        ],
        compiler_params=pltpu.CompilerParams(vmem_limit_bytes=VMEM_BYTES),
        cost_estimate=estimate(
            pairs * REP * chunk * chunk * HD * 10 * 4,
            queries.size * 6 + keys.size * 16,
            pairs * REP * chunk * chunk,
        ),
        name="attention_backward",
    )(qpos, kpos, lengths, queries, keys, values, attended, grads, lse, *before)


def rotate(vectors, cos_table, sin_table, back=False):
    heads = vectors.shape[0] // HD
    halves = vectors.reshape(heads, 2, HD // 2, vectors.shape[1])
    a, b = halves[:, 0], halves[:, 1]
    sin_table = -sin_table if back else sin_table
    turned = jnp.stack([a * cos_table - b * sin_table, b * cos_table + a * sin_table], axis=1)
    return turned.reshape(vectors.shape)


def contract(left, right, left_dim, right_dim):
    return lax.dot_general(
        left, right, (((left_dim,), (right_dim,)), ((), ())), preferred_element_type=f32
    )


def body(
    tokens_in, grad_out, seq_lengths, stretch_order, attn_gain, query_w, key_w, value_w,
    output_w, mlp_gain, gate_w, up_w, down_w,
):
    zs, ys = lax.axis_size("z"), lax.axis_size("y")
    z, c, y, x = (lax.axis_index(name) for name in ("z", "c", "y", "x"))
    rows, width = tokens_in.shape[1:]
    chunk = rows // 2
    unit = width // (zs * ys)

    def to_slots(value):
        if (unit // 2) % 128 == 0:
            return move_columns(value, y[None], zs, ys, True)
        parts = value.reshape(value.shape[0], zs, 2, ys, unit // 2)
        parts = [lax.dynamic_index_in_dim(parts, (y - k) % ys, 3) for k in range(ys)]
        return jnp.concatenate(
            [jnp.transpose(p, (0, 3, 1, 2, 4)).reshape(value.shape[0], width // ys) for p in parts],
            axis=1,
        )

    def from_slots(value):
        if (unit // 2) % 128 == 0:
            return move_columns(value, y[None], zs, ys, False)
        parts = value.reshape(value.shape[0], ys, zs, 2, unit // 2)
        parts = jnp.stack(
            [lax.dynamic_index_in_dim(parts, (y - k) % ys, 1, keepdims=False) for k in range(ys)], axis=3
        )
        return parts.reshape(value.shape[0], width)

    orders = jnp.stack([stretch_order[0], shift(stretch_order[0], "c", 1)])
    lengths = jnp.concatenate([seq_lengths, shift(seq_lengths, "c", 1)])
    slots = [
        2 * (((y - k) % ys) * 2 + (x if i == 0 else 1 - x)) + b
        for k in range(ys)
        for i in range(2)
        for b in range(2)
    ]
    kpos = jnp.stack([lax.dynamic_index_in_dim(orders, s, 1, keepdims=False) for s in slots], axis=1)
    qpos = kpos[:, :4]
    token_pos = (qpos[:, :, None] * chunk + jnp.arange(chunk, dtype=jnp.int32)).reshape(4 * rows)
    own_pos = token_pos[:rows]
    live = (own_pos < seq_lengths[0]).astype(f32)[:, None]
    angles = frequencies()[:, None] * token_pos.astype(f32)[None, :]
    cos_table, sin_table = jnp.cos(angles), jnp.sin(angles)

    gains = jnp.stack([attn_gain, mlp_gain])
    gains = in_order(gains, shift(gains, "x", 1), x, 1)
    gains = in_order(gains, shift(gains, "c", 1), c, 1)
    gains = gather_gains(gains).astype(f32)
    gain_one, gain_two = gains[0:1], gains[1:2]

    inputs = to_slots(tokens_in[0]).astype(f32)
    scale_one = lax.rsqrt(jnp.mean(inputs * inputs, axis=1, keepdims=True) + epsilon)
    unit_one = inputs * scale_one
    normed_own = (unit_one * gain_one).astype(bf16)

    def packed(*weights):
        return jnp.concatenate(
            [w[:, t * (w.shape[1] // 4) : (t + 1) * (w.shape[1] // 4)] for t in range(4) for w in weights],
            axis=1,
        )

    nq, nk = query_w.shape[1] // 4, key_w.shape[1] // 4
    nqkv = nq + 2 * nk
    attn_unit = spread_columns(packed(query_w, key_w, value_w, output_w), c, x)
    qkv_unit, out_unit = attn_unit[:, :nqkv], attn_unit[:, nqkv:]
    mlp_unit = spread_columns(packed(gate_w, up_w, down_w), c, x, (attn_unit,), (normed_own,))
    nf = gate_w.shape[1] // 4
    gate_unit, up_unit, down_unit = (mlp_unit[:, i * nf : (i + 1) * nf] for i in range(3))
    qkv_slots = gather_slots(gather_column(qkv_unit))
    own, beside, sibling, both_two = group_tokens(normed_own)
    out_column = hold(gather_column(hold(out_unit, normed_own)), beside)
    qkv_w = jnp.concatenate(qkv_slots, axis=0)
    out_slots = gather_slots(out_column)
    out_w = jnp.concatenate(out_slots, axis=0)
    gate_column = gather_column(hold(gate_unit, out_column))
    up_all, down_all = gather_whole(up_unit, y), gather_whole(down_unit, y)

    normed_one = jnp.concatenate([own, beside, sibling, both_two], axis=0)
    pre = contract(after(qkv_w, mlp_unit), normed_one, 0, 1)
    queries = (rotate(pre[:nq], cos_table, sin_table).astype(bf16)) * jnp.asarray(0.125, bf16)
    key_own = rotate(pre[nq : nq + nk], cos_table, sin_table).astype(bf16)
    value_own = pre[nq + nk :].astype(bf16)
    both_own = jnp.concatenate([key_own, value_own], axis=0)
    both = jnp.stack([both_own] + [shift(both_own, "y", k) for k in range(1, ys)])
    keys, values = both[:, :nk], both[:, nk:]
    gate_column = hold(gate_column, both)
    cut = gate_column.shape[0] // 2
    gate_first = [shift(gate_column[:cut], "y", k) for k in range(1, ys)]
    gate_rest = [shift(gate_column[cut:], "y", k) for k in range(1, ys)]
    grad_own = to_slots(grad_out[0]) * live.astype(bf16)
    grad_rows = grad_own.astype(f32)
    own, beside, sibling, both_two = group_tokens(hold(grad_own, both_own))
    grad_low = jnp.concatenate([own, sibling, both_two, beside], axis=0)

    attended_one, lse_one = attention_fwd(
        after(queries, grad_own, out_w), keys, values, qpos, kpos, lengths, chunk, 1
    )
    branch = contract(attended_one, out_w, 0, 1).astype(bf16)
    from_sibling = shift(branch[:rows], "c", 1)
    beside_sum = branch[rows:].astype(f32) + from_sibling.astype(f32)
    from_beside = shift(beside_sum.astype(bf16), "x", 1)
    attended_zero, lse_zero = attention_fwd(
        after(queries, from_sibling, both_two), keys, values, qpos, kpos, lengths, chunk, 0
    )
    branch = contract(after(attended_zero, from_beside, *gate_first), out_w, 0, 1).astype(bf16)
    middle = inputs + branch[:rows].astype(f32) + shift(branch[rows:], "c", 1).astype(f32) + from_beside.astype(f32)
    gate_all = [gate_column] + [jnp.concatenate(two, axis=0) for two in zip(gate_first, gate_rest)]
    attended = jnp.concatenate([attended_zero, attended_one], axis=1)
    scale_two = lax.rsqrt(jnp.mean(middle * middle, axis=1, keepdims=True) + epsilon)
    unit_two = middle * scale_two
    own, beside, sibling, both_two = group_tokens((unit_two * gain_two).astype(bf16))
    normed_two = jnp.concatenate([own, sibling, both_two, after(beside, *gate_rest)], axis=0)

    (gate_pre,) = rows_product(normed_two, gate_all, [], plain, 1, "gate")
    up_pre, hidden = rows_product(normed_two, up_all, [gate_pre], up_finish, 2, "up")

    def finish(total):
        return join_columns(total, c, x)

    by_y = (y - jnp.arange(ys, dtype=jnp.int32)) % ys
    last = columns_product(grad_low, by_y, ys, hidden, [], "down_grad")
    down_grad = scatter_whole(last)
    grad_gate, grad_up = rows_product(
        after(grad_low, last), down_all, [gate_pre, up_pre], hidden_back, 2, "hidden_grad"
    )
    norm_parts, last = [], grad_gate
    for g, u in zip(gate_all, up_all):
        last = turned_product([after(grad_gate, last), grad_up], [g, u], "norm_grad")
        norm_parts.append(last)
    sums = [scatter_by_c(part, False) for part in norm_parts]
    came = [shift(beside.astype(bf16), "x", 1) for _, beside in sums]
    last = columns_product(after(normed_two, last), by_y, ys, grad_gate, [], "gate_grad")
    gate_grad = scatter_whole(last)
    came[0] = after(came[0], last)
    last = columns_product(after(normed_two, last), by_y, ys, grad_up, [], "up_grad")
    up_grad = scatter_whole(last)
    came[-1] = after(came[-1], last)
    grad_norm_two = jnp.concatenate([mine + got.astype(f32) for (mine, _), got in zip(sums, came)], axis=1)
    gain_two_grad = jnp.sum(grad_norm_two * unit_two, axis=0)
    def gain_back(terms):
        own, other = halves(scatter_gains(terms, unit), c, 0)
        own, other = halves(own + shift(other, "c", 1), x, 0)
        return own + shift(other, "x", 1)

    scaled_two = grad_norm_two * gain_two
    grad_middle = grad_rows + scale_two * (
        scaled_two - unit_two * jnp.mean(scaled_two * unit_two, axis=1, keepdims=True)
    )

    def attn_terms(activations, grads, k):
        size = width // ys
        return contract(lax.dynamic_slice_in_dim(activations, k * size, size, 1), grads, 0, 1)

    own = grad_middle.astype(bf16)
    beside, sibling = shift(own, "x", 1), shift(own, "c", 1)
    grad_attn = contract(out_w, jnp.concatenate([own, sibling], axis=0), 0, 1).astype(bf16)
    query_zero, grad_keys, grad_values = attention_bwd(
        after(queries, down_grad), keys, values, attended_zero, grad_attn, lse_zero, qpos, kpos, lengths,
        chunk, 0,
    )
    beside = hold(beside, query_zero)
    both_two = shift(beside, "c", 1)
    branch_parts, last = [], query_zero
    for w in down_all:
        last = turned_product([after(hidden, last)], [w], "down")
        branch_parts.append(last)
    sent = [part[rows : 3 * rows] for part in branch_parts]
    got_c = [shift(part, "c", 1) for part in sent]
    down_own, down_got = join_by_c(hold(down_grad, query_zero), c)
    grad_attn = contract(out_w, jnp.concatenate([both_two, after(beside, last)], axis=0), 0, 1).astype(bf16)
    query_one, grad_keys, grad_values = attention_bwd(
        after(queries, down_got, *got_c), keys, values, attended_one, grad_attn, lse_one, qpos,
        kpos, lengths, chunk, 1, grad_keys, grad_values,
    )
    got_x = [
        shift((part[3 * rows :].astype(f32) + got[rows:].astype(f32)).astype(bf16), "x", 1)
        for part, got in zip(branch_parts, got_c)
    ]
    down_own, down_got = join_by_x(down_own, down_got, c, x)
    query_one = after(query_one, gate_grad, down_got, *got_x)
    down_grad = in_order(down_own, down_got, x, 1)
    branch_two = jnp.concatenate(
        [
            part[:rows].astype(f32) + from_c[:rows].astype(f32) + from_x.astype(f32)
            for part, from_c, from_x in zip(branch_parts, got_c, got_x)
        ],
        axis=1,
    )
    result = from_slots(((middle + branch_two) * live).astype(bf16))[None]
    grad_branch = jnp.concatenate([own, sibling, both_two, beside], axis=0)
    grad_branch = jnp.concatenate([own, sibling, both_two, beside], axis=0)
    gain_two_back = gain_back(hold(gain_two_grad, query_one))
    def pick(table, *chunks):
        return jnp.concatenate([table[:, i * rows : (i + 1) * rows] for i in chunks], axis=1)

    grad_both = jnp.concatenate([grad_keys, grad_values], axis=1)
    got = [shift(grad_both[k], "y", -k) for k in range(1, ys)]
    grad_both = sum([grad_both[0].astype(f32)] + [term.astype(f32) for term in got])
    turned_zero = rotate(query_zero, pick(cos_table, 0, 2), pick(sin_table, 0, 2), True).astype(bf16)
    turned_one = rotate(query_one, pick(cos_table, 3, 1), pick(sin_table, 3, 1), True).astype(bf16)
    grad_query = jnp.concatenate(
        [turned_zero[:, :rows], turned_one[:, rows:], turned_zero[:, rows:], turned_one[:, :rows]], axis=1
    )
    grad_qkv = jnp.concatenate(
        [
            grad_query,
            rotate(grad_both[:nk], cos_table, sin_table, True).astype(bf16),
            grad_both[nk:].astype(bf16),
        ],
        axis=0,
    )
    qkv_sent = send_slots([attn_terms(normed_one, grad_qkv, k).astype(bf16) for k in range(1, ys)])
    partial = contract(grad_qkv, qkv_w, 0, 1).astype(bf16)
    mine, beside_sum = scatter_by_c(partial, True)
    beside_sum = beside_sum.astype(bf16)
    from_beside = shift(beside_sum, "x", 1)
    gate_grad = finish(hold(gate_grad, from_beside))
    grad_norm_one = mine + from_beside.astype(f32)
    held = hold(attended, from_beside)
    output_grad = scatter_whole(
        jnp.concatenate([attn_terms(grad_branch, held, by_y[i]) for i in range(ys)], axis=0).astype(bf16)
    )
    qkv_grad = sum([attn_terms(normed_one, grad_qkv, 0)] + [t.astype(f32) for t in qkv_sent])
    qkv_grad = scatter_column(hold(qkv_grad.astype(bf16), up_grad, beside_sum))
    gain_one_grad = jnp.sum(grad_norm_one * unit_one, axis=0)
    scaled_one = grad_norm_one * gain_one
    up_grad = finish(hold(up_grad, from_beside))
    grad_inputs = grad_middle + scale_one * (
        scaled_one - unit_one * jnp.mean(scaled_one * unit_one, axis=1, keepdims=True)
    )

    qkv_back = finish(qkv_grad)

    def columns(low, high):
        return jnp.concatenate(
            [qkv_back[:, t * nqkv + low : t * nqkv + high] for t in range(4)], axis=1
        ).astype(f32)

    return (
        result,
        from_slots(grad_inputs)[None],
        gain_back(gain_one_grad),
        columns(0, nq),
        columns(nq, nq + nk),
        columns(nq + nk, nqkv),
        finish(output_grad).astype(f32),
        gain_two_back,
        gate_grad.astype(f32),
        up_grad.astype(f32),
        down_grad.astype(f32),
    )


def solution(mesh):
    dp, seq = mesh.shape["dp"], mesh.shape["seq"]
    fine = Mesh(mesh.devices.reshape(dp // 2, 2, seq // 2, 2), ("z", "c", "y", "x"))
    every = ("z", "c", "y", "x")
    tokens = P(("z", "c"), ("y", "x"), None)
    vector, matrix = P(every), P(every, None)
    return jax.shard_map(
        body,
        mesh=fine,
        in_specs=(
            tokens, tokens, P(("z", "c")), P(("z", "c"), None), vector, matrix, matrix, matrix,
            matrix, vector, matrix, matrix, matrix,
        ),
        out_specs=(
            tokens, tokens, vector, matrix, matrix, matrix, matrix, vector, matrix, matrix, matrix,
        ),
        check_vma=False,
    )
```

```python
import functools
import math

import jax
import jax.numpy as jnp
from jax import lax
from jax.experimental import pallas as pl
from jax.experimental.pallas import tpu as pltpu
from jax.sharding import Mesh
from jax.sharding import PartitionSpec as P

HEADS = 32
KVH = 8
HD = 64
REP = HEADS // KVH

epsilon = 1e-05
masked_score = -1e30
floor_score = -1e29

bf16 = jnp.bfloat16
f32 = jnp.float32


def frequencies():
    steps_even = jnp.arange(0, HD, 2).astype(f32) / HD
    base_freq = 1.0 / 500000.0**steps_even
    wavelength = 2.0 * math.pi / base_freq
    smooth = (8192.0 / wavelength - 1.0) / 3.0
    blended = (1.0 - smooth) * base_freq / 32.0 + smooth * base_freq
    return jnp.where(
        wavelength < 2048.0, base_freq, jnp.where(wavelength > 8192.0, base_freq / 32.0, blended)
    )


def shift(value, axis, steps):
    size = lax.axis_size(axis)
    return lax.ppermute(value, axis, [(i, (i + steps) % size) for i in range(size)])


def in_order(own, other, index, axis):
    return jnp.where(
        index == 0,
        jnp.concatenate([own, other], axis=axis),
        jnp.concatenate([other, own], axis=axis),
    )


def halves(value, index, axis):
    size = value.shape[axis] // 2
    return (
        lax.dynamic_slice_in_dim(value, index * size, size, axis),
        lax.dynamic_slice_in_dim(value, (1 - index) * size, size, axis),
    )


def spread_columns(shard, c, x, earlier=(), later=()):
    own, other = halves(shard, x, 1)
    if earlier:
        other = hold(other, *earlier)
    both = in_order(own, after(shift(other, "x", 1), *later), x, 0)
    own, other = halves(both, c, 1)
    return in_order(own, shift(other, "c", 1), c, 0)


def join_by_c(unit, c):
    own, other = halves(unit, c, 0)
    return own, shift(other, "c", 1)


def join_by_x(own, got, c, x):
    own, other = halves(in_order(own, got, c, 1), x, 0)
    return own, shift(other, "x", 1)


def join_columns(unit, c, x):
    own, got = join_by_x(*join_by_c(unit, c), c, x)
    return in_order(own, got, x, 1)


def after(value, *others):
    return lax.optimization_barrier((value,) + others)[0]


def hold_body(*refs):
    del refs


def hold(value, *others):
    return pl.pallas_call(
        hold_body,
        in_specs=[pl.BlockSpec(memory_space=pl.ANY)] * (1 + len(others)),
        out_specs=pl.BlockSpec(memory_space=pl.ANY),
        out_shape=jax.ShapeDtypeStruct(value.shape, value.dtype),
        input_output_aliases={0: 0},
        name="hold",
    )(value, *others)


def gather_column(unit):
    return lax.all_gather(unit, "z", axis=0, tiled=True)


def gather_slots(column):
    return [column] + [shift(column, "y", k) for k in range(1, lax.axis_size("y"))]


def send_slots(terms):
    return [shift(term, "y", -(k + 1)) for k, term in enumerate(terms)]


def gather_whole(unit, y):
    zs, ys = lax.axis_size("z"), lax.axis_size("y")
    size = zs * unit.shape[0]
    whole = lax.all_gather(unit, ("y", "z"), axis=0, tiled=True)
    return [lax.dynamic_slice_in_dim(whole, ((y - k) % ys) * size, size, 0) for k in range(ys)]


def scatter_whole(terms):
    return lax.psum_scatter(terms, ("y", "z"), scatter_dimension=0, tiled=True)


def scatter_column(total):
    return lax.psum_scatter(total, "z", scatter_dimension=0, tiled=True)


def gather_gains(unit):
    zs, ys = lax.axis_size("z"), lax.axis_size("y")
    row = jnp.stack([unit] + [shift(unit, "y", k) for k in range(1, ys)], axis=1)
    z = lax.axis_index("z")
    out = jnp.zeros((2, ys, zs, unit.shape[1]), unit.dtype)
    for j in range(zs):
        got = row if j == 0 else shift(row, "z", j)
        out = lax.dynamic_update_slice(out, got[:, :, None], (0, 0, (z - j) % zs, 0))
    return out.reshape(2, -1)


def scatter_gains(terms, unit):
    zs, ys = lax.axis_size("z"), lax.axis_size("y")
    z = lax.axis_index("z")
    terms = terms.reshape(ys, zs * unit)
    total = terms[0]
    for k in range(1, ys):
        total = total + shift(terms[k], "y", -k)
    total = total.reshape(zs, unit)
    out = lax.dynamic_index_in_dim(total, z, 0, keepdims=False)
    for j in range(1, zs):
        out = out + shift(lax.dynamic_index_in_dim(total, (z - j) % zs, 0, keepdims=False), "z", -j)
    return out


def group_tokens(own):
    beside = shift(own, "x", 1)
    return own, beside, shift(own, "c", 1), shift(beside, "c", 1)


def scatter_by_c(partial, by_sequence):
    count = partial.shape[0] // 4
    mine = partial[:count]
    if by_sequence:
        beside, sent = partial[count : 2 * count], partial[2 * count :]
    else:
        beside, sent = partial[3 * count :], partial[count : 3 * count]
    got = shift(sent, "c", 1).astype(f32)
    return mine.astype(f32) + got[:count], beside.astype(f32) + got[count:]


def scatter_tokens(partials, by_sequence):
    sums = []
    for partial in partials:
        mine, beside = scatter_by_c(partial, by_sequence)
        sums.append(mine + shift(beside.astype(bf16), "x", 1).astype(f32))
    return jnp.concatenate(sums, axis=1)


def move_columns_body(zs, ys, forth, y_ref, in_ref, out_ref):
    block = in_ref.shape[1] // (zs * 2 * ys)
    y = y_ref[0]
    for i in range(zs * 2):
        for k in range(ys):
            natural = i * ys + lax.rem(y - k + ys, ys)
            natural = pl.ds(pl.multiple_of(natural * block, block), block)
            slot = pl.ds((k * zs * 2 + i) * block, block)
            if forth:
                out_ref[:, slot] = in_ref[:, natural]
            else:
                out_ref[:, natural] = in_ref[:, slot]


def move_columns(value, y, zs, ys, forth):
    rows, width = value.shape
    tall = rows // 4
    spec = pl.BlockSpec((tall, width), lambda i, *_: (i, 0))
    return pl.pallas_call(
        functools.partial(move_columns_body, zs, ys, forth),
        grid_spec=pltpu.PrefetchScalarGridSpec(
            num_scalar_prefetch=1, grid=(4,), in_specs=[spec], out_specs=spec
        ),
        out_shape=jax.ShapeDtypeStruct(value.shape, value.dtype),
        cost_estimate=pl.CostEstimate(
            flops=0, bytes_accessed=2 * value.size * value.dtype.itemsize, transcendentals=0
        ),
        name="move_columns",
    )(y, value)


VMEM_BYTES = 56 * 1024 * 1024
EASE = 1


def estimate(flops, moved, exps=0):
    return pl.CostEstimate(
        flops=int(flops) // EASE, bytes_accessed=int(moved) // EASE, transcendentals=int(exps) // EASE
    )


def fit(size, most):
    return size if size <= most else fit(size // 2, most)


def rows_product(left, parts, extras, finish, n_out, name):
    t, d = left.shape
    n = parts[0].shape[1]
    depth = parts[0].shape[0]
    bm, bn = fit(t, 512), fit(n, 1024)
    n_parts, n_extra = len(parts), len(extras)

    def kernel(*refs):
        left_ref = refs[0]
        product = None
        for p in range(n_parts):
            term = jnp.dot(
                left_ref[:, p * depth : (p + 1) * depth], refs[1 + p][...], preferred_element_type=f32
            )
            product = term if product is None else product + term
        got = finish(product, *(r[...] for r in refs[1 + n_parts : 1 + n_parts + n_extra]))
        for ref, value in zip(refs[1 + n_parts + n_extra :], got):
            ref[...] = value.astype(bf16)

    tile = pl.BlockSpec((bm, bn), lambda j, i: (i, j))
    return pl.pallas_call(
        kernel,
        grid=(n // bn, t // bm),
        in_specs=[pl.BlockSpec((bm, d), lambda j, i: (i, 0))]
        + [pl.BlockSpec((depth, bn), lambda j, i: (0, j))] * n_parts
        + [tile] * n_extra,
        out_specs=[tile] * n_out,
        out_shape=[jax.ShapeDtypeStruct((t, n), bf16)] * n_out,
        compiler_params=pltpu.CompilerParams(vmem_limit_bytes=VMEM_BYTES),
        cost_estimate=estimate(2 * t * d * n, 2 * (t * d + d * n + t * n)),
        name=name,
    )(left, *parts, *extras)


def turned_product(lefts, rights, name):
    t, f = lefts[0].shape
    n = rights[0].shape[0]
    bm, bn = fit(t, 512), fit(n, 1024)
    count = len(lefts)

    def kernel(*refs):
        product = None
        for p in range(count):
            term = lax.dot_general(
                refs[p][...], refs[count + p][...], (((1,), (1,)), ((), ())), preferred_element_type=f32
            )
            product = term if product is None else product + term
        refs[2 * count][...] = product.astype(bf16)

    return pl.pallas_call(
        kernel,
        grid=(n // bn, t // bm),
        in_specs=[pl.BlockSpec((bm, f), lambda j, i: (i, 0))] * count
        + [pl.BlockSpec((bn, f), lambda j, i: (j, 0))] * count,
        out_specs=pl.BlockSpec((bm, bn), lambda j, i: (i, j)),
        out_shape=jax.ShapeDtypeStruct((t, n), bf16),
        compiler_params=pltpu.CompilerParams(vmem_limit_bytes=VMEM_BYTES),
        cost_estimate=estimate(2 * count * t * f * n, 2 * count * (t * f + f * n)),
        name=name,
    )(*lefts, *rights)


def columns_product(left, slots, n_parts, right, others, name):
    t, d = left.shape
    m = d // n_parts
    f = right.shape[1]
    bm, bn = fit(m, 512), fit(f, 1024)
    per = m // bm
    count = len(others)

    def kernel(slots_ref, left_ref, right_ref, *refs):
        turned_ref = refs[-1]

        @pl.when(pl.program_id(1) == 0)
        def _():
            turned_ref[...] = left_ref[...].T

        product = jnp.dot(turned_ref[...], right_ref[...], preferred_element_type=f32)
        for ref in refs[:count]:
            product = product + ref[...].astype(f32)
        refs[count][...] = product.astype(bf16)

    rows = slots.shape[0] * m
    tile = pl.BlockSpec((bm, bn), lambda i, j, slots_ref: (i, j))
    return pl.pallas_call(
        kernel,
        grid_spec=pltpu.PrefetchScalarGridSpec(
            num_scalar_prefetch=1,
            grid=(rows // bm, f // bn),
            in_specs=[
                pl.BlockSpec((t, bm), lambda i, j, slots_ref: (0, slots_ref[i // per] * per + i % per)),
                pl.BlockSpec((t, bn), lambda i, j, slots_ref: (0, j)),
            ]
            + [tile] * count,
            out_specs=tile,
            scratch_shapes=[pltpu.VMEM((bm, t), bf16)],
        ),
        out_shape=jax.ShapeDtypeStruct((rows, f), bf16),
        compiler_params=pltpu.CompilerParams(vmem_limit_bytes=VMEM_BYTES),
        cost_estimate=estimate(2 * t * rows * f, 2 * (t * m + t * f + rows * f)),
        name=name,
    )(slots, left, right, *others)


def plain(product):
    return (product,)


def up_finish(product, gate):
    gate = gate.astype(f32)
    return product, gate * jax.nn.sigmoid(gate) * product


def hidden_back(grad, gate, up):
    gate, up = gate.astype(f32), up.astype(f32)
    sigmoid = jax.nn.sigmoid(gate)
    return grad * up * sigmoid * (1.0 + gate * (1.0 - sigmoid)), grad * gate * sigmoid


def seen(chunk, first, qp, length):
    shape = (chunk, REP * chunk)
    at_key = first + lax.broadcasted_iota(jnp.int32, shape, 0)
    at_query = qp * chunk + (lax.broadcasted_iota(jnp.int32, shape, 1) & (chunk - 1))
    return (at_key <= at_query) & (at_key < length)


def attention_fwd_body(
    chunk, blocks, part, qpos_ref, kpos_ref, len_ref, q_ref, k_ref, v_ref, o_ref, lse_ref,
    kn_ref, q4_ref, m_ref, l_ref, acc_ref,
):
    s, qb = pl.program_id(0), pl.program_id(2)
    ys = k_ref.shape[0]

    @pl.when(qb == 0)
    def _():
        for yk in range(ys):
            for b in range(blocks):
                kn_ref[pl.ds((yk * blocks + b) * chunk, chunk), :] = (
                    k_ref[yk, :, pl.ds(b * chunk, chunk)].astype(f32).T.astype(bf16)
                )

    qp = qpos_ref[s, part * (blocks // 2) + qb]
    length = len_ref[s]
    for h in range(REP):
        q4_ref[:, h * chunk : (h + 1) * chunk] = q_ref[h * HD : (h + 1) * HD, :]
    m_ref[...] = jnp.full_like(m_ref, floor_score)
    l_ref[...] = jnp.zeros_like(l_ref)
    acc_ref[...] = jnp.zeros_like(acc_ref)

    for yk in range(ys):

        def step(b, carry, yk=yk):
            kp = kpos_ref[s, yk * blocks + b]
            first = kp * chunk
            live = (kp <= qp) & (first < length)
            partly = (kp == qp) | (first + chunk > length)

            def work(masked):
                kn = kn_ref[pl.ds(pl.multiple_of((yk * blocks + b) * chunk, chunk), chunk), :]
                vt = v_ref[yk, :, pl.ds(pl.multiple_of(b * chunk, chunk), chunk)]
                scores = jnp.dot(kn, q4_ref[...], preferred_element_type=f32)
                if masked:
                    scores = jnp.where(seen(chunk, first, qp, length), scores, masked_score)
                m_old = m_ref[...]
                m_new = jnp.maximum(m_old, jnp.max(scores, axis=0, keepdims=True))
                alpha = jnp.exp(m_old - m_new)
                probs = jnp.exp(scores - m_new)
                m_ref[...] = m_new
                l_ref[...] = l_ref[...] * alpha + jnp.sum(probs, axis=0, keepdims=True)
                acc_ref[...] = acc_ref[...] * alpha + jnp.dot(
                    vt, probs.astype(bf16), preferred_element_type=f32
                )

            pl.when(live & partly)(lambda: work(True))
            pl.when(live & jnp.logical_not(partly))(lambda: work(False))
            return carry

        lax.fori_loop(0, blocks, step, 0)

    out = (acc_ref[...] / l_ref[...]).astype(bf16)
    lse = m_ref[...] + jnp.log(l_ref[...])
    for h in range(REP):
        columns = slice(h * chunk, (h + 1) * chunk)
        o_ref[h * HD : (h + 1) * HD, :] = out[:, columns]
        lse_ref[0, h : h + 1, :] = lse[:, columns]


def attention_fwd(queries, keys, values, qpos, kpos, lengths, chunk, part):
    tokens = queries.shape[1]
    groups = queries.shape[0] // (REP * HD)
    ys = keys.shape[0]
    half = tokens // 2
    blocks = half // chunk
    few = blocks // 2
    q_spec = pl.BlockSpec((REP * HD, chunk), lambda s, g, b, *_: (g, s * blocks + part * few + b))
    o_spec = pl.BlockSpec((REP * HD, chunk), lambda s, g, b, *_: (g, ((s + part) % 2) * few + b))
    kv_spec = pl.BlockSpec((ys, HD, half), lambda s, g, b, *_: (0, g, s))
    lse_spec = pl.BlockSpec((1, REP, chunk), lambda s, g, b, *_: (g, 0, ((s + part) % 2) * few + b))
    pairs = 2 * groups * few * blocks * ys
    return pl.pallas_call(
        functools.partial(attention_fwd_body, chunk, blocks, part),
        grid_spec=pltpu.PrefetchScalarGridSpec(
            num_scalar_prefetch=3,
            grid=(2, groups, few),
            in_specs=[q_spec, kv_spec, kv_spec],
            out_specs=[o_spec, lse_spec],
            scratch_shapes=[
                pltpu.VMEM((ys * half, HD), bf16),
                pltpu.VMEM((HD, REP * chunk), bf16),
                pltpu.VMEM((1, REP * chunk), f32),
                pltpu.VMEM((1, REP * chunk), f32),
                pltpu.VMEM((HD, REP * chunk), f32),
            ],
        ),
        compiler_params=pltpu.CompilerParams(vmem_limit_bytes=VMEM_BYTES),
        out_shape=[
            jax.ShapeDtypeStruct((queries.shape[0], half), bf16),
            jax.ShapeDtypeStruct((groups, REP, half), f32),
        ],
        cost_estimate=estimate(
            pairs * REP * chunk * chunk * HD * 4 * 8,
            queries.size * 2 + keys.size * 4,
            pairs * REP * chunk * chunk,
        ),
        name="attention_forward",
    )(qpos, kpos, lengths, queries, keys, values)


def attention_bwd_body(
    chunk, blocks, part, n_before, qpos_ref, kpos_ref, len_ref, q_ref, k_ref, v_ref, o_ref, do_ref,
    lse_ref, *refs,
):
    before = refs[:n_before]
    dq_ref, dk_ref, dv_ref, kn_ref, vn_ref, q4_ref, do4_ref, dqa_ref, dka_ref, dva_ref, row_ref = refs[n_before:]
    s, qb = pl.program_id(0), pl.program_id(2)
    ys = k_ref.shape[0]

    @pl.when(qb == 0)
    def _():
        if before:
            dka_ref[...] = before[0][...]
            dva_ref[...] = before[1][...]
        else:
            dka_ref[...] = jnp.zeros_like(dka_ref)
            dva_ref[...] = jnp.zeros_like(dva_ref)
        for yk in range(ys):
            for b in range(blocks):
                rows = pl.ds((yk * blocks + b) * chunk, chunk)
                cols = pl.ds(b * chunk, chunk)
                kn_ref[rows, :] = k_ref[yk, :, cols].astype(f32).T.astype(bf16)
                vn_ref[rows, :] = v_ref[yk, :, cols].astype(f32).T.astype(bf16)

    qp = qpos_ref[s, part * (blocks // 2) + qb]
    length = len_ref[s]
    dqa_ref[...] = jnp.zeros_like(dqa_ref)
    for h in range(REP):
        rows, columns = slice(h * HD, (h + 1) * HD), slice(h * chunk, (h + 1) * chunk)
        q4_ref[:, columns] = q_ref[rows, :]
        do4_ref[:, columns] = do_ref[rows, :]
        row_ref[0:1, columns] = lse_ref[0, h : h + 1, :]
        row_ref[1:2, columns] = jnp.sum(
            do_ref[rows, :].astype(f32) * o_ref[rows, :].astype(f32), axis=0, keepdims=True
        )

    for yk in range(ys):

        def step(b, carry, yk=yk):
            kp = kpos_ref[s, yk * blocks + b]
            first = kp * chunk
            live = (kp <= qp) & (first < length)
            partly = (kp == qp) | (first + chunk > length)

            def work(masked):
                at = pl.ds(pl.multiple_of((yk * blocks + b) * chunk, chunk), chunk)
                cols = pl.ds(pl.multiple_of(b * chunk, chunk), chunk)
                q4, do4 = q4_ref[...], do4_ref[...]
                scores = jnp.dot(kn_ref[at, :], q4, preferred_element_type=f32)
                if masked:
                    scores = jnp.where(seen(chunk, first, qp, length), scores, masked_score)
                probs = jnp.exp(scores - row_ref[0:1, :])
                grad_probs = jnp.dot(vn_ref[at, :], do4, preferred_element_type=f32)
                grad_scores = (probs * (grad_probs - row_ref[1:2, :])).astype(bf16)
                across = (((1,), (1,)), ((), ()))
                dva_ref[yk, :, cols] += lax.dot_general(
                    do4, probs.astype(bf16), across, preferred_element_type=f32
                )
                dqa_ref[...] += jnp.dot(k_ref[yk, :, cols], grad_scores, preferred_element_type=f32)
                dka_ref[yk, :, cols] += lax.dot_general(
                    q4, grad_scores, across, preferred_element_type=f32
                )

            pl.when(live & partly)(lambda: work(True))
            pl.when(live & jnp.logical_not(partly))(lambda: work(False))
            return carry

        lax.fori_loop(0, blocks, step, 0)

    for h in range(REP):
        dq_ref[h * HD : (h + 1) * HD, :] = dqa_ref[:, h * chunk : (h + 1) * chunk] * 0.125

    @pl.when(qb == blocks // 2 - 1)
    def _():
        dk_ref[...] = dka_ref[...].astype(dk_ref.dtype)
        dv_ref[...] = dva_ref[...].astype(dv_ref.dtype)


def attention_bwd(queries, keys, values, attended, grads, lse, qpos, kpos, lengths, chunk, part, *before):
    tokens = queries.shape[1]
    groups = queries.shape[0] // (REP * HD)
    ys = keys.shape[0]
    half = tokens // 2
    blocks = half // chunk
    few = blocks // 2
    q_spec = pl.BlockSpec((REP * HD, chunk), lambda s, g, b, *_: (g, s * blocks + part * few + b))
    o_spec = pl.BlockSpec((REP * HD, chunk), lambda s, g, b, *_: (g, ((s + part) % 2) * few + b))
    kv_spec = pl.BlockSpec((ys, HD, half), lambda s, g, b, *_: (0, g, s))
    lse_spec = pl.BlockSpec((1, REP, chunk), lambda s, g, b, *_: (g, 0, ((s + part) % 2) * few + b))
    pairs = 2 * groups * few * blocks * ys
    kind = bf16 if before else f32
    return pl.pallas_call(
        functools.partial(attention_bwd_body, chunk, blocks, part, len(before)),
        grid_spec=pltpu.PrefetchScalarGridSpec(
            num_scalar_prefetch=3,
            grid=(2, groups, few),
            in_specs=[q_spec, kv_spec, kv_spec, o_spec, o_spec, lse_spec] + [kv_spec] * len(before),
            out_specs=[o_spec, kv_spec, kv_spec],
            scratch_shapes=[
                pltpu.VMEM((ys * half, HD), bf16),
                pltpu.VMEM((ys * half, HD), bf16),
                pltpu.VMEM((HD, REP * chunk), bf16),
                pltpu.VMEM((HD, REP * chunk), bf16),
                pltpu.VMEM((HD, REP * chunk), f32),
                pltpu.VMEM((ys, HD, half), f32),
                pltpu.VMEM((ys, HD, half), f32),
                pltpu.VMEM((2, REP * chunk), f32),
            ],
        ),
        out_shape=[
            jax.ShapeDtypeStruct((queries.shape[0], half), f32),
            jax.ShapeDtypeStruct(keys.shape, kind),
            jax.ShapeDtypeStruct(keys.shape, kind),
        ],
        compiler_params=pltpu.CompilerParams(vmem_limit_bytes=VMEM_BYTES),
        cost_estimate=estimate(
            pairs * REP * chunk * chunk * HD * 10 * 4,
            queries.size * 6 + keys.size * 16,
            pairs * REP * chunk * chunk,
        ),
        name="attention_backward",
    )(qpos, kpos, lengths, queries, keys, values, attended, grads, lse, *before)


def rotate(vectors, cos_table, sin_table, back=False):
    heads = vectors.shape[0] // HD
    halves = vectors.reshape(heads, 2, HD // 2, vectors.shape[1])
    a, b = halves[:, 0], halves[:, 1]
    sin_table = -sin_table if back else sin_table
    turned = jnp.stack([a * cos_table - b * sin_table, b * cos_table + a * sin_table], axis=1)
    return turned.reshape(vectors.shape)


def contract(left, right, left_dim, right_dim):
    return lax.dot_general(
        left, right, (((left_dim,), (right_dim,)), ((), ())), preferred_element_type=f32
    )


def body(
    tokens_in, grad_out, seq_lengths, stretch_order, attn_gain, query_w, key_w, value_w,
    output_w, mlp_gain, gate_w, up_w, down_w,
):
    zs, ys = lax.axis_size("z"), lax.axis_size("y")
    z, c, y, x = (lax.axis_index(name) for name in ("z", "c", "y", "x"))
    rows, width = tokens_in.shape[1:]
    chunk = rows // 2
    unit = width // (zs * ys)

    def to_slots(value):
        if (unit // 2) % 128 == 0:
            return move_columns(value, y[None], zs, ys, True)
        parts = value.reshape(value.shape[0], zs, 2, ys, unit // 2)
        parts = [lax.dynamic_index_in_dim(parts, (y - k) % ys, 3) for k in range(ys)]
        return jnp.concatenate(
            [jnp.transpose(p, (0, 3, 1, 2, 4)).reshape(value.shape[0], width // ys) for p in parts],
            axis=1,
        )

    def from_slots(value):
        if (unit // 2) % 128 == 0:
            return move_columns(value, y[None], zs, ys, False)
        parts = value.reshape(value.shape[0], ys, zs, 2, unit // 2)
        parts = jnp.stack(
            [lax.dynamic_index_in_dim(parts, (y - k) % ys, 1, keepdims=False) for k in range(ys)], axis=3
        )
        return parts.reshape(value.shape[0], width)

    orders = jnp.stack([stretch_order[0], shift(stretch_order[0], "c", 1)])
    lengths = jnp.concatenate([seq_lengths, shift(seq_lengths, "c", 1)])
    slots = [
        2 * (((y - k) % ys) * 2 + (x if i == 0 else 1 - x)) + b
        for k in range(ys)
        for i in range(2)
        for b in range(2)
    ]
    kpos = jnp.stack([lax.dynamic_index_in_dim(orders, s, 1, keepdims=False) for s in slots], axis=1)
    qpos = kpos[:, :4]
    token_pos = (qpos[:, :, None] * chunk + jnp.arange(chunk, dtype=jnp.int32)).reshape(4 * rows)
    own_pos = token_pos[:rows]
    live = (own_pos < seq_lengths[0]).astype(f32)[:, None]
    angles = frequencies()[:, None] * token_pos.astype(f32)[None, :]
    cos_table, sin_table = jnp.cos(angles), jnp.sin(angles)

    gains = jnp.stack([attn_gain, mlp_gain])
    gains = in_order(gains, shift(gains, "x", 1), x, 1)
    gains = in_order(gains, shift(gains, "c", 1), c, 1)
    gains = gather_gains(gains).astype(f32)
    gain_one, gain_two = gains[0:1], gains[1:2]

    inputs = to_slots(tokens_in[0]).astype(f32)
    scale_one = lax.rsqrt(jnp.mean(inputs * inputs, axis=1, keepdims=True) + epsilon)
    unit_one = inputs * scale_one
    normed_own = (unit_one * gain_one).astype(bf16)

    def packed(*weights):
        return jnp.concatenate(
            [w[:, t * (w.shape[1] // 4) : (t + 1) * (w.shape[1] // 4)] for t in range(4) for w in weights],
            axis=1,
        )

    nq, nk = query_w.shape[1] // 4, key_w.shape[1] // 4
    nqkv = nq + 2 * nk
    attn_unit = spread_columns(packed(query_w, key_w, value_w, output_w), c, x)
    qkv_unit, out_unit = attn_unit[:, :nqkv], attn_unit[:, nqkv:]
    mlp_unit = spread_columns(packed(gate_w, up_w, down_w), c, x, (attn_unit,), (normed_own,))
    nf = gate_w.shape[1] // 4
    gate_unit, up_unit, down_unit = (mlp_unit[:, i * nf : (i + 1) * nf] for i in range(3))
    qkv_slots = gather_slots(gather_column(qkv_unit))
    own, beside, sibling, both_two = group_tokens(normed_own)
    out_column = hold(gather_column(hold(out_unit, normed_own)), beside)
    qkv_w = jnp.concatenate(qkv_slots, axis=0)
    out_slots = gather_slots(out_column)
    out_w = jnp.concatenate(out_slots, axis=0)
    gate_column = gather_column(hold(gate_unit, out_column))
    up_all, down_all = gather_whole(up_unit, y), gather_whole(down_unit, y)

    normed_one = jnp.concatenate([own, beside, sibling, both_two], axis=0)
    pre = contract(after(qkv_w, mlp_unit), normed_one, 0, 1)
    queries = (rotate(pre[:nq], cos_table, sin_table).astype(bf16)) * jnp.asarray(0.125, bf16)
    key_own = rotate(pre[nq : nq + nk], cos_table, sin_table).astype(bf16)
    value_own = pre[nq + nk :].astype(bf16)
    both_own = jnp.concatenate([key_own, value_own], axis=0)
    both = jnp.stack([both_own] + [shift(both_own, "y", k) for k in range(1, ys)])
    keys, values = both[:, :nk], both[:, nk:]
    gate_column = hold(gate_column, both)
    cut = gate_column.shape[0] // 2
    gate_first = [shift(gate_column[:cut], "y", k) for k in range(1, ys)]
    gate_rest = [shift(gate_column[cut:], "y", k) for k in range(1, ys)]
    grad_own = to_slots(grad_out[0]) * live.astype(bf16)
    grad_rows = grad_own.astype(f32)
    own, beside, sibling, both_two = group_tokens(hold(grad_own, both_own))
    grad_low = jnp.concatenate([own, sibling, both_two, beside], axis=0)

    attended_one, lse_one = attention_fwd(
        after(queries, grad_own, out_w), keys, values, qpos, kpos, lengths, chunk, 1
    )
    branch = contract(attended_one, out_w, 0, 1).astype(bf16)
    from_sibling = shift(branch[:rows], "c", 1)
    beside_sum = branch[rows:].astype(f32) + from_sibling.astype(f32)
    from_beside = shift(beside_sum.astype(bf16), "x", 1)
    attended_zero, lse_zero = attention_fwd(
        after(queries, from_sibling, both_two), keys, values, qpos, kpos, lengths, chunk, 0
    )
    branch = contract(after(attended_zero, from_beside, *gate_first), out_w, 0, 1).astype(bf16)
    middle = inputs + branch[:rows].astype(f32) + shift(branch[rows:], "c", 1).astype(f32) + from_beside.astype(f32)
    gate_all = [gate_column] + [jnp.concatenate(two, axis=0) for two in zip(gate_first, gate_rest)]
    attended = jnp.concatenate([attended_zero, attended_one], axis=1)
    scale_two = lax.rsqrt(jnp.mean(middle * middle, axis=1, keepdims=True) + epsilon)
    unit_two = middle * scale_two
    own, beside, sibling, both_two = group_tokens((unit_two * gain_two).astype(bf16))
    normed_two = jnp.concatenate([own, sibling, both_two, after(beside, *gate_rest)], axis=0)

    (gate_pre,) = rows_product(normed_two, gate_all, [], plain, 1, "gate")
    up_pre, hidden = rows_product(normed_two, up_all, [gate_pre], up_finish, 2, "up")

    def finish(total):
        return join_columns(total, c, x)

    by_y = (y - jnp.arange(ys, dtype=jnp.int32)) % ys
    last = columns_product(grad_low, by_y, ys, hidden, [], "down_grad")
    down_grad = scatter_whole(last)
    grad_gate, grad_up = rows_product(
        after(grad_low, last), down_all, [gate_pre, up_pre], hidden_back, 2, "hidden_grad"
    )
    norm_parts, last = [], grad_gate
    for g, u in zip(gate_all, up_all):
        last = turned_product([after(grad_gate, last), grad_up], [g, u], "norm_grad")
        norm_parts.append(last)
    sums = [scatter_by_c(part, False) for part in norm_parts]
    came = [shift(beside.astype(bf16), "x", 1) for _, beside in sums]
    last = columns_product(after(normed_two, last), by_y, ys, grad_gate, [], "gate_grad")
    gate_grad = scatter_whole(last)
    came[0] = after(came[0], last)
    last = columns_product(after(normed_two, last), by_y, ys, grad_up, [], "up_grad")
    up_grad = scatter_whole(last)
    came[-1] = after(came[-1], last)
    grad_norm_two = jnp.concatenate([mine + got.astype(f32) for (mine, _), got in zip(sums, came)], axis=1)
    gain_two_grad = jnp.sum(grad_norm_two * unit_two, axis=0)
    def gain_back(terms):
        own, other = halves(scatter_gains(terms, unit), c, 0)
        own, other = halves(own + shift(other, "c", 1), x, 0)
        return own + shift(other, "x", 1)

    scaled_two = grad_norm_two * gain_two
    grad_middle = grad_rows + scale_two * (
        scaled_two - unit_two * jnp.mean(scaled_two * unit_two, axis=1, keepdims=True)
    )

    def attn_terms(activations, grads, k):
        size = width // ys
        return contract(lax.dynamic_slice_in_dim(activations, k * size, size, 1), grads, 0, 1)

    own = grad_middle.astype(bf16)
    beside, sibling = shift(own, "x", 1), shift(own, "c", 1)
    grad_attn = contract(out_w, jnp.concatenate([own, sibling], axis=0), 0, 1).astype(bf16)
    query_zero, grad_keys, grad_values = attention_bwd(
        after(queries, down_grad), keys, values, attended_zero, grad_attn, lse_zero, qpos, kpos, lengths,
        chunk, 0,
    )
    beside = hold(beside, query_zero)
    both_two = shift(beside, "c", 1)
    branch_parts, last = [], query_zero
    for w in down_all:
        last = turned_product([after(hidden, last)], [w], "down")
        branch_parts.append(last)
    sent = [part[rows : 3 * rows] for part in branch_parts]
    got_c = [shift(part, "c", 1) for part in sent]
    down_own, down_got = join_by_c(hold(down_grad, query_zero), c)
    grad_attn = contract(out_w, jnp.concatenate([both_two, after(beside, last)], axis=0), 0, 1).astype(bf16)
    query_one, grad_keys, grad_values = attention_bwd(
        after(queries, down_got, *got_c), keys, values, attended_one, grad_attn, lse_one, qpos,
        kpos, lengths, chunk, 1, grad_keys, grad_values,
    )
    got_x = [
        shift((part[3 * rows :].astype(f32) + got[rows:].astype(f32)).astype(bf16), "x", 1)
        for part, got in zip(branch_parts, got_c)
    ]
    down_own, down_got = join_by_x(down_own, down_got, c, x)
    query_one = after(query_one, gate_grad, down_got, *got_x)
    down_grad = in_order(down_own, down_got, x, 1)
    branch_two = jnp.concatenate(
        [
            part[:rows].astype(f32) + from_c[:rows].astype(f32) + from_x.astype(f32)
            for part, from_c, from_x in zip(branch_parts, got_c, got_x)
        ],
        axis=1,
    )
    result = from_slots(((middle + branch_two) * live).astype(bf16))[None]
    grad_branch = jnp.concatenate([own, sibling, both_two, beside], axis=0)
    grad_branch = jnp.concatenate([own, sibling, both_two, beside], axis=0)
    gain_two_back = gain_back(hold(gain_two_grad, query_one))
    def pick(table, *chunks):
        return jnp.concatenate([table[:, i * rows : (i + 1) * rows] for i in chunks], axis=1)

    grad_both = jnp.concatenate([grad_keys, grad_values], axis=1)
    got = [shift(grad_both[k], "y", -k) for k in range(1, ys)]
    grad_both = sum([grad_both[0].astype(f32)] + [term.astype(f32) for term in got])
    turned_zero = rotate(query_zero, pick(cos_table, 0, 2), pick(sin_table, 0, 2), True).astype(bf16)
    turned_one = rotate(query_one, pick(cos_table, 3, 1), pick(sin_table, 3, 1), True).astype(bf16)
    grad_query = jnp.concatenate(
        [turned_zero[:, :rows], turned_one[:, rows:], turned_zero[:, rows:], turned_one[:, :rows]], axis=1
    )
    grad_qkv = jnp.concatenate(
        [
            grad_query,
            rotate(grad_both[:nk], cos_table, sin_table, True).astype(bf16),
            grad_both[nk:].astype(bf16),
        ],
        axis=0,
    )
    qkv_sent = send_slots([attn_terms(normed_one, grad_qkv, k).astype(bf16) for k in range(1, ys)])
    partial = contract(grad_qkv, qkv_w, 0, 1).astype(bf16)
    mine, beside_sum = scatter_by_c(partial, True)
    beside_sum = beside_sum.astype(bf16)
    from_beside = shift(beside_sum, "x", 1)
    gate_grad = finish(hold(gate_grad, from_beside))
    grad_norm_one = mine + from_beside.astype(f32)
    held = hold(attended, beside_sum)
    output_grad = scatter_whole(
        jnp.concatenate([attn_terms(grad_branch, held, by_y[i]) for i in range(ys)], axis=0).astype(bf16)
    )
    qkv_grad = sum([attn_terms(normed_one, grad_qkv, 0)] + [t.astype(f32) for t in qkv_sent])
    qkv_grad = scatter_column(hold(qkv_grad.astype(bf16), up_grad, beside_sum))
    gain_one_grad = jnp.sum(grad_norm_one * unit_one, axis=0)
    scaled_one = grad_norm_one * gain_one
    up_grad = finish(hold(up_grad, from_beside))
    grad_inputs = grad_middle + scale_one * (
        scaled_one - unit_one * jnp.mean(scaled_one * unit_one, axis=1, keepdims=True)
    )

    qkv_back = finish(qkv_grad)

    def columns(low, high):
        return jnp.concatenate(
            [qkv_back[:, t * nqkv + low : t * nqkv + high] for t in range(4)], axis=1
        ).astype(f32)

    return (
        result,
        from_slots(grad_inputs)[None],
        gain_back(gain_one_grad),
        columns(0, nq),
        columns(nq, nq + nk),
        columns(nq + nk, nqkv),
        finish(output_grad).astype(f32),
        gain_two_back,
        gate_grad.astype(f32),
        up_grad.astype(f32),
        down_grad.astype(f32),
    )


def solution(mesh):
    dp, seq = mesh.shape["dp"], mesh.shape["seq"]
    fine = Mesh(mesh.devices.reshape(dp // 2, 2, seq // 2, 2), ("z", "c", "y", "x"))
    every = ("z", "c", "y", "x")
    tokens = P(("z", "c"), ("y", "x"), None)
    vector, matrix = P(every), P(every, None)
    return jax.shard_map(
        body,
        mesh=fine,
        in_specs=(
            tokens, tokens, P(("z", "c")), P(("z", "c"), None), vector, matrix, matrix, matrix,
            matrix, vector, matrix, matrix, matrix,
        ),
        out_specs=(
            tokens, tokens, vector, matrix, matrix, matrix, matrix, vector, matrix, matrix, matrix,
        ),
        check_vma=False,
    )
```

```python
import functools
import math

import jax
import jax.numpy as jnp
from jax import lax
from jax.experimental import pallas as pl
from jax.experimental.pallas import tpu as pltpu
from jax.sharding import Mesh
from jax.sharding import PartitionSpec as P

HEADS = 32
KVH = 8
HD = 64
REP = HEADS // KVH

epsilon = 1e-05
masked_score = -1e30
floor_score = -1e29

bf16 = jnp.bfloat16
f32 = jnp.float32


def frequencies():
    steps_even = jnp.arange(0, HD, 2).astype(f32) / HD
    base_freq = 1.0 / 500000.0**steps_even
    wavelength = 2.0 * math.pi / base_freq
    smooth = (8192.0 / wavelength - 1.0) / 3.0
    blended = (1.0 - smooth) * base_freq / 32.0 + smooth * base_freq
    return jnp.where(
        wavelength < 2048.0, base_freq, jnp.where(wavelength > 8192.0, base_freq / 32.0, blended)
    )


def shift(value, axis, steps):
    size = lax.axis_size(axis)
    return lax.ppermute(value, axis, [(i, (i + steps) % size) for i in range(size)])


def in_order(own, other, index, axis):
    return jnp.where(
        index == 0,
        jnp.concatenate([own, other], axis=axis),
        jnp.concatenate([other, own], axis=axis),
    )


def halves(value, index, axis):
    size = value.shape[axis] // 2
    return (
        lax.dynamic_slice_in_dim(value, index * size, size, axis),
        lax.dynamic_slice_in_dim(value, (1 - index) * size, size, axis),
    )


def spread_columns(shard, c, x, earlier=(), later=()):
    own, other = halves(shard, x, 1)
    if earlier:
        other = hold(other, *earlier)
    both = in_order(own, after(shift(other, "x", 1), *later), x, 0)
    own, other = halves(both, c, 1)
    return in_order(own, shift(other, "c", 1), c, 0)


def join_by_c(unit, c):
    own, other = halves(unit, c, 0)
    return own, shift(other, "c", 1)


def join_by_x(own, got, c, x):
    own, other = halves(in_order(own, got, c, 1), x, 0)
    return own, shift(other, "x", 1)


def join_columns(unit, c, x):
    own, got = join_by_x(*join_by_c(unit, c), c, x)
    return in_order(own, got, x, 1)


def after(value, *others):
    return lax.optimization_barrier((value,) + others)[0]


def hold_body(*refs):
    del refs


def hold(value, *others):
    return pl.pallas_call(
        hold_body,
        in_specs=[pl.BlockSpec(memory_space=pl.ANY)] * (1 + len(others)),
        out_specs=pl.BlockSpec(memory_space=pl.ANY),
        out_shape=jax.ShapeDtypeStruct(value.shape, value.dtype),
        input_output_aliases={0: 0},
        name="hold",
    )(value, *others)


def gather_column(unit):
    return lax.all_gather(unit, "z", axis=0, tiled=True)


def gather_slots(column):
    return [column] + [shift(column, "y", k) for k in range(1, lax.axis_size("y"))]


def send_slots(terms):
    return [shift(term, "y", -(k + 1)) for k, term in enumerate(terms)]


def gather_whole(unit):
    return lax.all_gather(unit, ("y", "z"), axis=0, tiled=True)


def scatter_whole(terms):
    return lax.psum_scatter(terms, ("y", "z"), scatter_dimension=0, tiled=True)


def scatter_column(total):
    return lax.psum_scatter(total, "z", scatter_dimension=0, tiled=True)


def gather_gains(unit):
    zs, ys = lax.axis_size("z"), lax.axis_size("y")
    row = jnp.stack([unit] + [shift(unit, "y", k) for k in range(1, ys)], axis=1)
    z = lax.axis_index("z")
    out = jnp.zeros((2, ys, zs, unit.shape[1]), unit.dtype)
    for j in range(zs):
        got = row if j == 0 else shift(row, "z", j)
        out = lax.dynamic_update_slice(out, got[:, :, None], (0, 0, (z - j) % zs, 0))
    return out.reshape(2, -1)


def scatter_gains(terms, unit):
    zs, ys = lax.axis_size("z"), lax.axis_size("y")
    z = lax.axis_index("z")
    terms = terms.reshape(ys, zs * unit)
    total = terms[0]
    for k in range(1, ys):
        total = total + shift(terms[k], "y", -k)
    total = total.reshape(zs, unit)
    out = lax.dynamic_index_in_dim(total, z, 0, keepdims=False)
    for j in range(1, zs):
        out = out + shift(lax.dynamic_index_in_dim(total, (z - j) % zs, 0, keepdims=False), "z", -j)
    return out


def group_tokens(own):
    beside = shift(own, "x", 1)
    return own, beside, shift(own, "c", 1), shift(beside, "c", 1)


def scatter_by_c(partial, by_sequence):
    count = partial.shape[0] // 4
    mine = partial[:count]
    if by_sequence:
        beside, sent = partial[count : 2 * count], partial[2 * count :]
    else:
        beside, sent = partial[3 * count :], partial[count : 3 * count]
    got = shift(sent, "c", 1).astype(f32)
    return mine.astype(f32) + got[:count], beside.astype(f32) + got[count:]


def scatter_tokens(partials, by_sequence):
    sums = []
    for partial in partials:
        mine, beside = scatter_by_c(partial, by_sequence)
        sums.append(mine + shift(beside.astype(bf16), "x", 1).astype(f32))
    return jnp.concatenate(sums, axis=1)


def move_columns_body(zs, ys, forth, y_ref, in_ref, out_ref):
    block = in_ref.shape[1] // (zs * 2 * ys)
    y = y_ref[0]
    for i in range(zs * 2):
        for k in range(ys):
            natural = i * ys + lax.rem(y - k + ys, ys)
            natural = pl.ds(pl.multiple_of(natural * block, block), block)
            slot = pl.ds((k * zs * 2 + i) * block, block)
            if forth:
                out_ref[:, slot] = in_ref[:, natural]
            else:
                out_ref[:, natural] = in_ref[:, slot]


def move_columns(value, y, zs, ys, forth):
    rows, width = value.shape
    tall = rows // 4
    spec = pl.BlockSpec((tall, width), lambda i, *_: (i, 0))
    return pl.pallas_call(
        functools.partial(move_columns_body, zs, ys, forth),
        grid_spec=pltpu.PrefetchScalarGridSpec(
            num_scalar_prefetch=1, grid=(4,), in_specs=[spec], out_specs=spec
        ),
        out_shape=jax.ShapeDtypeStruct(value.shape, value.dtype),
        cost_estimate=pl.CostEstimate(
            flops=0, bytes_accessed=2 * value.size * value.dtype.itemsize, transcendentals=0
        ),
        name="move_columns",
    )(y, value)


VMEM_BYTES = 56 * 1024 * 1024
EASE = 1


def estimate(flops, moved, exps=0):
    return pl.CostEstimate(
        flops=int(flops) // EASE, bytes_accessed=int(moved) // EASE, transcendentals=int(exps) // EASE
    )


def fit(size, most):
    return size if size <= most else fit(size // 2, most)


def rows_product(left, parts, places, extras, finish, n_out, name):
    t, d = left.shape
    n = parts[0].shape[1]
    depth = d // len(parts)
    bm, bn = fit(t, 512), fit(n, 1024)
    n_parts, n_extra = len(parts), len(extras)

    def kernel(places_ref, *refs):
        del places_ref
        left_ref = refs[0]
        product = None
        for p in range(n_parts):
            term = jnp.dot(
                left_ref[:, p * depth : (p + 1) * depth], refs[1 + p][...], preferred_element_type=f32
            )
            product = term if product is None else product + term
        got = finish(product, *(r[...] for r in refs[1 + n_parts : 1 + n_parts + n_extra]))
        for ref, value in zip(refs[1 + n_parts + n_extra :], got):
            ref[...] = value.astype(bf16)

    tile = pl.BlockSpec((bm, bn), lambda j, i, w: (i, j))
    return pl.pallas_call(
        kernel,
        grid_spec=pltpu.PrefetchScalarGridSpec(
            num_scalar_prefetch=1,
            grid=(n // bn, t // bm),
            in_specs=[pl.BlockSpec((bm, d), lambda j, i, w: (i, 0))]
            + [pl.BlockSpec((depth, bn), lambda j, i, w, p=p: (w[p], j)) for p in range(n_parts)]
            + [tile] * n_extra,
            out_specs=[tile] * n_out,
        ),
        out_shape=[jax.ShapeDtypeStruct((t, n), bf16)] * n_out,
        compiler_params=pltpu.CompilerParams(vmem_limit_bytes=VMEM_BYTES),
        cost_estimate=estimate(2 * t * d * n, 2 * (t * d + d * n + t * n)),
        name=name,
    )(places, left, *parts, *extras)


def turned_product(lefts, rights, places, n, name):
    t, f = lefts[0].shape
    bm, bn = fit(t, 512), fit(n, 1024)
    count = len(lefts)

    def kernel(places_ref, *refs):
        del places_ref
        product = None
        for p in range(count):
            term = lax.dot_general(
                refs[p][...], refs[count + p][...], (((1,), (1,)), ((), ())), preferred_element_type=f32
            )
            product = term if product is None else product + term
        refs[2 * count][...] = product.astype(bf16)

    return pl.pallas_call(
        kernel,
        grid_spec=pltpu.PrefetchScalarGridSpec(
            num_scalar_prefetch=1,
            grid=(n // bn, t // bm),
            in_specs=[pl.BlockSpec((bm, f), lambda j, i, w: (i, 0))] * count
            + [pl.BlockSpec((bn, f), lambda j, i, w, p=p: (w[p] * (n // bn) + j, 0)) for p in range(count)],
            out_specs=pl.BlockSpec((bm, bn), lambda j, i, w: (i, j)),
        ),
        out_shape=jax.ShapeDtypeStruct((t, n), bf16),
        compiler_params=pltpu.CompilerParams(vmem_limit_bytes=VMEM_BYTES),
        cost_estimate=estimate(2 * count * t * f * n, 2 * count * (t * f + f * n)),
        name=name,
    )(places, *lefts, *rights)


def columns_product(left, slots, n_parts, right, others, name):
    t, d = left.shape
    m = d // n_parts
    f = right.shape[1]
    bm, bn = fit(m, 512), fit(f, 1024)
    per = m // bm
    count = len(others)

    def kernel(slots_ref, left_ref, right_ref, *refs):
        turned_ref = refs[-1]

        @pl.when(pl.program_id(1) == 0)
        def _():
            turned_ref[...] = left_ref[...].T

        product = jnp.dot(turned_ref[...], right_ref[...], preferred_element_type=f32)
        for ref in refs[:count]:
            product = product + ref[...].astype(f32)
        refs[count][...] = product.astype(bf16)

    rows = slots.shape[0] * m
    tile = pl.BlockSpec((bm, bn), lambda i, j, slots_ref: (i, j))
    return pl.pallas_call(
        kernel,
        grid_spec=pltpu.PrefetchScalarGridSpec(
            num_scalar_prefetch=1,
            grid=(rows // bm, f // bn),
            in_specs=[
                pl.BlockSpec((t, bm), lambda i, j, slots_ref: (0, slots_ref[i // per] * per + i % per)),
                pl.BlockSpec((t, bn), lambda i, j, slots_ref: (0, j)),
            ]
            + [tile] * count,
            out_specs=tile,
            scratch_shapes=[pltpu.VMEM((bm, t), bf16)],
        ),
        out_shape=jax.ShapeDtypeStruct((rows, f), bf16),
        compiler_params=pltpu.CompilerParams(vmem_limit_bytes=VMEM_BYTES),
        cost_estimate=estimate(2 * t * rows * f, 2 * (t * m + t * f + rows * f)),
        name=name,
    )(slots, left, right, *others)


def plain(product):
    return (product,)


def up_finish(product, gate):
    gate = gate.astype(f32)
    return product, gate * jax.nn.sigmoid(gate) * product


def hidden_back(grad, gate, up):
    gate, up = gate.astype(f32), up.astype(f32)
    sigmoid = jax.nn.sigmoid(gate)
    return grad * up * sigmoid * (1.0 + gate * (1.0 - sigmoid)), grad * gate * sigmoid


def seen(chunk, first, qp, length):
    shape = (chunk, REP * chunk)
    at_key = first + lax.broadcasted_iota(jnp.int32, shape, 0)
    at_query = qp * chunk + (lax.broadcasted_iota(jnp.int32, shape, 1) & (chunk - 1))
    return (at_key <= at_query) & (at_key < length)


def attention_fwd_body(
    chunk, blocks, part, qpos_ref, kpos_ref, len_ref, q_ref, k_ref, v_ref, o_ref, lse_ref,
    kn_ref, q4_ref, m_ref, l_ref, acc_ref,
):
    s, qb = pl.program_id(0), pl.program_id(2)
    ys = k_ref.shape[0]

    @pl.when(qb == 0)
    def _():
        for yk in range(ys):
            for b in range(blocks):
                kn_ref[pl.ds((yk * blocks + b) * chunk, chunk), :] = (
                    k_ref[yk, :, pl.ds(b * chunk, chunk)].astype(f32).T.astype(bf16)
                )

    qp = qpos_ref[s, part * (blocks // 2) + qb]
    length = len_ref[s]
    for h in range(REP):
        q4_ref[:, h * chunk : (h + 1) * chunk] = q_ref[h * HD : (h + 1) * HD, :]
    m_ref[...] = jnp.full_like(m_ref, floor_score)
    l_ref[...] = jnp.zeros_like(l_ref)
    acc_ref[...] = jnp.zeros_like(acc_ref)

    for yk in range(ys):

        def step(b, carry, yk=yk):
            kp = kpos_ref[s, yk * blocks + b]
            first = kp * chunk
            live = (kp <= qp) & (first < length)
            partly = (kp == qp) | (first + chunk > length)

            def work(masked):
                kn = kn_ref[pl.ds(pl.multiple_of((yk * blocks + b) * chunk, chunk), chunk), :]
                vt = v_ref[yk, :, pl.ds(pl.multiple_of(b * chunk, chunk), chunk)]
                scores = jnp.dot(kn, q4_ref[...], preferred_element_type=f32)
                if masked:
                    scores = jnp.where(seen(chunk, first, qp, length), scores, masked_score)
                m_old = m_ref[...]
                m_new = jnp.maximum(m_old, jnp.max(scores, axis=0, keepdims=True))
                alpha = jnp.exp(m_old - m_new)
                probs = jnp.exp(scores - m_new)
                m_ref[...] = m_new
                l_ref[...] = l_ref[...] * alpha + jnp.sum(probs, axis=0, keepdims=True)
                acc_ref[...] = acc_ref[...] * alpha + jnp.dot(
                    vt, probs.astype(bf16), preferred_element_type=f32
                )

            pl.when(live & partly)(lambda: work(True))
            pl.when(live & jnp.logical_not(partly))(lambda: work(False))
            return carry

        lax.fori_loop(0, blocks, step, 0)

    out = (acc_ref[...] / l_ref[...]).astype(bf16)
    lse = m_ref[...] + jnp.log(l_ref[...])
    for h in range(REP):
        columns = slice(h * chunk, (h + 1) * chunk)
        o_ref[h * HD : (h + 1) * HD, :] = out[:, columns]
        lse_ref[0, h : h + 1, :] = lse[:, columns]


def attention_fwd(queries, keys, values, qpos, kpos, lengths, chunk, part):
    tokens = queries.shape[1]
    groups = queries.shape[0] // (REP * HD)
    ys = keys.shape[0]
    half = tokens // 2
    blocks = half // chunk
    few = blocks // 2
    q_spec = pl.BlockSpec((REP * HD, chunk), lambda s, g, b, *_: (g, s * blocks + part * few + b))
    o_spec = pl.BlockSpec((REP * HD, chunk), lambda s, g, b, *_: (g, ((s + part) % 2) * few + b))
    kv_spec = pl.BlockSpec((ys, HD, half), lambda s, g, b, *_: (0, g, s))
    lse_spec = pl.BlockSpec((1, REP, chunk), lambda s, g, b, *_: (g, 0, ((s + part) % 2) * few + b))
    pairs = 2 * groups * few * blocks * ys
    return pl.pallas_call(
        functools.partial(attention_fwd_body, chunk, blocks, part),
        grid_spec=pltpu.PrefetchScalarGridSpec(
            num_scalar_prefetch=3,
            grid=(2, groups, few),
            in_specs=[q_spec, kv_spec, kv_spec],
            out_specs=[o_spec, lse_spec],
            scratch_shapes=[
                pltpu.VMEM((ys * half, HD), bf16),
                pltpu.VMEM((HD, REP * chunk), bf16),
                pltpu.VMEM((1, REP * chunk), f32),
                pltpu.VMEM((1, REP * chunk), f32),
                pltpu.VMEM((HD, REP * chunk), f32),
            ],
        ),
        compiler_params=pltpu.CompilerParams(vmem_limit_bytes=VMEM_BYTES),
        out_shape=[
            jax.ShapeDtypeStruct((queries.shape[0], half), bf16),
            jax.ShapeDtypeStruct((groups, REP, half), f32),
        ],
        cost_estimate=estimate(
            pairs * REP * chunk * chunk * HD * 4 * 8,
            queries.size * 2 + keys.size * 4,
            pairs * REP * chunk * chunk,
        ),
        name="attention_forward",
    )(qpos, kpos, lengths, queries, keys, values)


def attention_bwd_body(
    chunk, blocks, part, n_before, qpos_ref, kpos_ref, len_ref, q_ref, k_ref, v_ref, o_ref, do_ref,
    lse_ref, *refs,
):
    before = refs[:n_before]
    dq_ref, dk_ref, dv_ref, kn_ref, vn_ref, q4_ref, do4_ref, dqa_ref, dka_ref, dva_ref, row_ref = refs[n_before:]
    s, qb = pl.program_id(0), pl.program_id(2)
    ys = k_ref.shape[0]

    @pl.when(qb == 0)
    def _():
        if before:
            dka_ref[...] = before[0][...]
            dva_ref[...] = before[1][...]
        else:
            dka_ref[...] = jnp.zeros_like(dka_ref)
            dva_ref[...] = jnp.zeros_like(dva_ref)
        for yk in range(ys):
            for b in range(blocks):
                rows = pl.ds((yk * blocks + b) * chunk, chunk)
                cols = pl.ds(b * chunk, chunk)
                kn_ref[rows, :] = k_ref[yk, :, cols].astype(f32).T.astype(bf16)
                vn_ref[rows, :] = v_ref[yk, :, cols].astype(f32).T.astype(bf16)

    qp = qpos_ref[s, part * (blocks // 2) + qb]
    length = len_ref[s]
    dqa_ref[...] = jnp.zeros_like(dqa_ref)
    for h in range(REP):
        rows, columns = slice(h * HD, (h + 1) * HD), slice(h * chunk, (h + 1) * chunk)
        q4_ref[:, columns] = q_ref[rows, :]
        do4_ref[:, columns] = do_ref[rows, :]
        row_ref[0:1, columns] = lse_ref[0, h : h + 1, :]
        row_ref[1:2, columns] = jnp.sum(
            do_ref[rows, :].astype(f32) * o_ref[rows, :].astype(f32), axis=0, keepdims=True
        )

    for yk in range(ys):

        def step(b, carry, yk=yk):
            kp = kpos_ref[s, yk * blocks + b]
            first = kp * chunk
            live = (kp <= qp) & (first < length)
            partly = (kp == qp) | (first + chunk > length)

            def work(masked):
                at = pl.ds(pl.multiple_of((yk * blocks + b) * chunk, chunk), chunk)
                cols = pl.ds(pl.multiple_of(b * chunk, chunk), chunk)
                q4, do4 = q4_ref[...], do4_ref[...]
                scores = jnp.dot(kn_ref[at, :], q4, preferred_element_type=f32)
                if masked:
                    scores = jnp.where(seen(chunk, first, qp, length), scores, masked_score)
                probs = jnp.exp(scores - row_ref[0:1, :])
                grad_probs = jnp.dot(vn_ref[at, :], do4, preferred_element_type=f32)
                grad_scores = (probs * (grad_probs - row_ref[1:2, :])).astype(bf16)
                across = (((1,), (1,)), ((), ()))
                dva_ref[yk, :, cols] += lax.dot_general(
                    do4, probs.astype(bf16), across, preferred_element_type=f32
                )
                dqa_ref[...] += jnp.dot(k_ref[yk, :, cols], grad_scores, preferred_element_type=f32)
                dka_ref[yk, :, cols] += lax.dot_general(
                    q4, grad_scores, across, preferred_element_type=f32
                )

            pl.when(live & partly)(lambda: work(True))
            pl.when(live & jnp.logical_not(partly))(lambda: work(False))
            return carry

        lax.fori_loop(0, blocks, step, 0)

    for h in range(REP):
        dq_ref[h * HD : (h + 1) * HD, :] = dqa_ref[:, h * chunk : (h + 1) * chunk] * 0.125

    @pl.when(qb == blocks // 2 - 1)
    def _():
        dk_ref[...] = dka_ref[...].astype(dk_ref.dtype)
        dv_ref[...] = dva_ref[...].astype(dv_ref.dtype)


def attention_bwd(queries, keys, values, attended, grads, lse, qpos, kpos, lengths, chunk, part, *before):
    tokens = queries.shape[1]
    groups = queries.shape[0] // (REP * HD)
    ys = keys.shape[0]
    half = tokens // 2
    blocks = half // chunk
    few = blocks // 2
    q_spec = pl.BlockSpec((REP * HD, chunk), lambda s, g, b, *_: (g, s * blocks + part * few + b))
    o_spec = pl.BlockSpec((REP * HD, chunk), lambda s, g, b, *_: (g, ((s + part) % 2) * few + b))
    kv_spec = pl.BlockSpec((ys, HD, half), lambda s, g, b, *_: (0, g, s))
    lse_spec = pl.BlockSpec((1, REP, chunk), lambda s, g, b, *_: (g, 0, ((s + part) % 2) * few + b))
    pairs = 2 * groups * few * blocks * ys
    kind = bf16 if before else f32
    return pl.pallas_call(
        functools.partial(attention_bwd_body, chunk, blocks, part, len(before)),
        grid_spec=pltpu.PrefetchScalarGridSpec(
            num_scalar_prefetch=3,
            grid=(2, groups, few),
            in_specs=[q_spec, kv_spec, kv_spec, o_spec, o_spec, lse_spec] + [kv_spec] * len(before),
            out_specs=[o_spec, kv_spec, kv_spec],
            scratch_shapes=[
                pltpu.VMEM((ys * half, HD), bf16),
                pltpu.VMEM((ys * half, HD), bf16),
                pltpu.VMEM((HD, REP * chunk), bf16),
                pltpu.VMEM((HD, REP * chunk), bf16),
                pltpu.VMEM((HD, REP * chunk), f32),
                pltpu.VMEM((ys, HD, half), f32),
                pltpu.VMEM((ys, HD, half), f32),
                pltpu.VMEM((2, REP * chunk), f32),
            ],
        ),
        out_shape=[
            jax.ShapeDtypeStruct((queries.shape[0], half), f32),
            jax.ShapeDtypeStruct(keys.shape, kind),
            jax.ShapeDtypeStruct(keys.shape, kind),
        ],
        compiler_params=pltpu.CompilerParams(vmem_limit_bytes=VMEM_BYTES),
        cost_estimate=estimate(
            pairs * REP * chunk * chunk * HD * 10 * 4,
            queries.size * 6 + keys.size * 16,
            pairs * REP * chunk * chunk,
        ),
        name="attention_backward",
    )(qpos, kpos, lengths, queries, keys, values, attended, grads, lse, *before)


def rotate(vectors, cos_table, sin_table, back=False):
    heads = vectors.shape[0] // HD
    halves = vectors.reshape(heads, 2, HD // 2, vectors.shape[1])
    a, b = halves[:, 0], halves[:, 1]
    sin_table = -sin_table if back else sin_table
    turned = jnp.stack([a * cos_table - b * sin_table, b * cos_table + a * sin_table], axis=1)
    return turned.reshape(vectors.shape)


def contract(left, right, left_dim, right_dim):
    return lax.dot_general(
        left, right, (((left_dim,), (right_dim,)), ((), ())), preferred_element_type=f32
    )


def body(
    tokens_in, grad_out, seq_lengths, stretch_order, attn_gain, query_w, key_w, value_w,
    output_w, mlp_gain, gate_w, up_w, down_w,
):
    zs, ys = lax.axis_size("z"), lax.axis_size("y")
    z, c, y, x = (lax.axis_index(name) for name in ("z", "c", "y", "x"))
    rows, width = tokens_in.shape[1:]
    chunk = rows // 2
    unit = width // (zs * ys)

    def to_slots(value):
        if (unit // 2) % 128 == 0:
            return move_columns(value, y[None], zs, ys, True)
        parts = value.reshape(value.shape[0], zs, 2, ys, unit // 2)
        parts = [lax.dynamic_index_in_dim(parts, (y - k) % ys, 3) for k in range(ys)]
        return jnp.concatenate(
            [jnp.transpose(p, (0, 3, 1, 2, 4)).reshape(value.shape[0], width // ys) for p in parts],
            axis=1,
        )

    def from_slots(value):
        if (unit // 2) % 128 == 0:
            return move_columns(value, y[None], zs, ys, False)
        parts = value.reshape(value.shape[0], ys, zs, 2, unit // 2)
        parts = jnp.stack(
            [lax.dynamic_index_in_dim(parts, (y - k) % ys, 1, keepdims=False) for k in range(ys)], axis=3
        )
        return parts.reshape(value.shape[0], width)

    orders = jnp.stack([stretch_order[0], shift(stretch_order[0], "c", 1)])
    lengths = jnp.concatenate([seq_lengths, shift(seq_lengths, "c", 1)])
    slots = [
        2 * (((y - k) % ys) * 2 + (x if i == 0 else 1 - x)) + b
        for k in range(ys)
        for i in range(2)
        for b in range(2)
    ]
    kpos = jnp.stack([lax.dynamic_index_in_dim(orders, s, 1, keepdims=False) for s in slots], axis=1)
    qpos = kpos[:, :4]
    token_pos = (qpos[:, :, None] * chunk + jnp.arange(chunk, dtype=jnp.int32)).reshape(4 * rows)
    own_pos = token_pos[:rows]
    live = (own_pos < seq_lengths[0]).astype(f32)[:, None]
    angles = frequencies()[:, None] * token_pos.astype(f32)[None, :]
    cos_table, sin_table = jnp.cos(angles), jnp.sin(angles)

    gains = jnp.stack([attn_gain, mlp_gain])
    gains = in_order(gains, shift(gains, "x", 1), x, 1)
    gains = in_order(gains, shift(gains, "c", 1), c, 1)
    gains = gather_gains(gains).astype(f32)
    gain_one, gain_two = gains[0:1], gains[1:2]

    inputs = to_slots(tokens_in[0]).astype(f32)
    scale_one = lax.rsqrt(jnp.mean(inputs * inputs, axis=1, keepdims=True) + epsilon)
    unit_one = inputs * scale_one
    normed_own = (unit_one * gain_one).astype(bf16)

    def packed(*weights):
        return jnp.concatenate(
            [w[:, t * (w.shape[1] // 4) : (t + 1) * (w.shape[1] // 4)] for t in range(4) for w in weights],
            axis=1,
        )

    nq, nk = query_w.shape[1] // 4, key_w.shape[1] // 4
    nqkv = nq + 2 * nk
    attn_unit = spread_columns(packed(query_w, key_w, value_w, output_w), c, x)
    qkv_unit, out_unit = attn_unit[:, :nqkv], attn_unit[:, nqkv:]
    mlp_unit = spread_columns(packed(gate_w, up_w, down_w), c, x, (attn_unit,), (normed_own,))
    nf = gate_w.shape[1] // 4
    gate_unit, up_unit, down_unit = (mlp_unit[:, i * nf : (i + 1) * nf] for i in range(3))
    qkv_slots = gather_slots(gather_column(qkv_unit))
    own, beside, sibling, both_two = group_tokens(normed_own)
    out_column = hold(gather_column(hold(out_unit, normed_own)), beside)
    qkv_w = jnp.concatenate(qkv_slots, axis=0)
    out_slots = gather_slots(out_column)
    out_w = jnp.concatenate(out_slots, axis=0)
    gate_column = gather_column(hold(gate_unit, out_column))
    up_all, down_all = gather_whole(up_unit), gather_whole(down_unit)

    normed_one = jnp.concatenate([own, beside, sibling, both_two], axis=0)
    pre = contract(after(qkv_w, mlp_unit), normed_one, 0, 1)
    queries = (rotate(pre[:nq], cos_table, sin_table).astype(bf16)) * jnp.asarray(0.125, bf16)
    key_own = rotate(pre[nq : nq + nk], cos_table, sin_table).astype(bf16)
    value_own = pre[nq + nk :].astype(bf16)
    both_own = jnp.concatenate([key_own, value_own], axis=0)
    both = jnp.stack([both_own] + [shift(both_own, "y", k) for k in range(1, ys)])
    keys, values = both[:, :nk], both[:, nk:]
    gate_column = hold(gate_column, both)
    cut = gate_column.shape[0] // 2
    gate_first = [shift(gate_column[:cut], "y", k) for k in range(1, ys)]
    gate_rest = [shift(gate_column[cut:], "y", k) for k in range(1, ys)]
    grad_own = to_slots(grad_out[0]) * live.astype(bf16)
    grad_rows = grad_own.astype(f32)
    own, beside, sibling, both_two = group_tokens(hold(grad_own, both_own))
    grad_low = jnp.concatenate([own, sibling, both_two, beside], axis=0)

    attended_one, lse_one = attention_fwd(
        after(queries, grad_own, out_w), keys, values, qpos, kpos, lengths, chunk, 1
    )
    branch = contract(attended_one, out_w, 0, 1).astype(bf16)
    from_sibling = shift(branch[:rows], "c", 1)
    beside_sum = branch[rows:].astype(f32) + from_sibling.astype(f32)
    from_beside = shift(beside_sum.astype(bf16), "x", 1)
    attended_zero, lse_zero = attention_fwd(
        after(queries, from_sibling, both_two), keys, values, qpos, kpos, lengths, chunk, 0
    )
    branch = contract(after(attended_zero, from_beside, *gate_first), out_w, 0, 1).astype(bf16)
    middle = inputs + branch[:rows].astype(f32) + shift(branch[rows:], "c", 1).astype(f32) + from_beside.astype(f32)
    gate_all = [gate_column] + [jnp.concatenate(two, axis=0) for two in zip(gate_first, gate_rest)]
    attended = jnp.concatenate([attended_zero, attended_one], axis=1)
    scale_two = lax.rsqrt(jnp.mean(middle * middle, axis=1, keepdims=True) + epsilon)
    unit_two = middle * scale_two
    own, beside, sibling, both_two = group_tokens((unit_two * gain_two).astype(bf16))
    normed_two = jnp.concatenate([own, sibling, both_two, after(beside, *gate_rest)], axis=0)

    by_y = (y - jnp.arange(ys, dtype=jnp.int32)) % ys
    at_start = jnp.zeros((ys,), jnp.int32)
    part_rows = width // ys
    (gate_pre,) = rows_product(normed_two, gate_all, at_start, [], plain, 1, "gate")
    up_pre, hidden = rows_product(normed_two, [up_all] * ys, by_y, [gate_pre], up_finish, 2, "up")

    def finish(total):
        return join_columns(total, c, x)

    last = columns_product(grad_low, by_y, ys, hidden, [], "down_grad")
    down_grad = scatter_whole(last)
    grad_gate, grad_up = rows_product(
        after(grad_low, last), [down_all] * ys, by_y, [gate_pre, up_pre], hidden_back, 2, "hidden_grad"
    )
    norm_parts, last = [], grad_gate
    for k, g in enumerate(gate_all):
        places = jnp.stack([at_start[k], by_y[k]])
        last = turned_product([after(grad_gate, last), grad_up], [g, up_all], places, part_rows, "norm_grad")
        norm_parts.append(last)
    sums = [scatter_by_c(part, False) for part in norm_parts]
    came = [shift(beside.astype(bf16), "x", 1) for _, beside in sums]
    last = columns_product(after(normed_two, last), by_y, ys, grad_gate, [], "gate_grad")
    gate_grad = scatter_whole(last)
    came[0] = after(came[0], last)
    last = columns_product(after(normed_two, last), by_y, ys, grad_up, [], "up_grad")
    up_grad = scatter_whole(last)
    came[-1] = after(came[-1], last)
    grad_norm_two = jnp.concatenate([mine + got.astype(f32) for (mine, _), got in zip(sums, came)], axis=1)
    gain_two_grad = jnp.sum(grad_norm_two * unit_two, axis=0)
    def gain_back(terms):
        own, other = halves(scatter_gains(terms, unit), c, 0)
        own, other = halves(own + shift(other, "c", 1), x, 0)
        return own + shift(other, "x", 1)

    scaled_two = grad_norm_two * gain_two
    grad_middle = grad_rows + scale_two * (
        scaled_two - unit_two * jnp.mean(scaled_two * unit_two, axis=1, keepdims=True)
    )

    def attn_terms(activations, grads, k):
        size = width // ys
        return contract(lax.dynamic_slice_in_dim(activations, k * size, size, 1), grads, 0, 1)

    own = grad_middle.astype(bf16)
    beside, sibling = shift(own, "x", 1), shift(own, "c", 1)
    grad_attn = contract(out_w, jnp.concatenate([own, sibling], axis=0), 0, 1).astype(bf16)
    query_zero, grad_keys, grad_values = attention_bwd(
        after(queries, down_grad), keys, values, attended_zero, grad_attn, lse_zero, qpos, kpos, lengths,
        chunk, 0,
    )
    beside = hold(beside, query_zero)
    both_two = shift(beside, "c", 1)
    branch_parts, last = [], query_zero
    for k in range(ys):
        last = turned_product([after(hidden, last)], [down_all], by_y[k][None], part_rows, "down")
        branch_parts.append(last)
    sent = [part[rows : 3 * rows] for part in branch_parts]
    got_c = [shift(part, "c", 1) for part in sent]
    down_own, down_got = join_by_c(hold(down_grad, query_zero), c)
    grad_attn = contract(out_w, jnp.concatenate([both_two, after(beside, last)], axis=0), 0, 1).astype(bf16)
    query_one, grad_keys, grad_values = attention_bwd(
        after(queries, down_got, *got_c), keys, values, attended_one, grad_attn, lse_one, qpos,
        kpos, lengths, chunk, 1, grad_keys, grad_values,
    )
    got_x = [
        shift((part[3 * rows :].astype(f32) + got[rows:].astype(f32)).astype(bf16), "x", 1)
        for part, got in zip(branch_parts, got_c)
    ]
    down_own, down_got = join_by_x(down_own, down_got, c, x)
    query_one = after(query_one, gate_grad, down_got, *got_x)
    down_grad = in_order(down_own, down_got, x, 1)
    branch_two = jnp.concatenate(
        [
            part[:rows].astype(f32) + from_c[:rows].astype(f32) + from_x.astype(f32)
            for part, from_c, from_x in zip(branch_parts, got_c, got_x)
        ],
        axis=1,
    )
    result = from_slots(((middle + branch_two) * live).astype(bf16))[None]
    grad_branch = jnp.concatenate([own, sibling, both_two, beside], axis=0)
    grad_branch = jnp.concatenate([own, sibling, both_two, beside], axis=0)
    gain_two_back = gain_back(hold(gain_two_grad, query_one))
    def pick(table, *chunks):
        return jnp.concatenate([table[:, i * rows : (i + 1) * rows] for i in chunks], axis=1)

    grad_both = jnp.concatenate([grad_keys, grad_values], axis=1)
    got = [shift(grad_both[k], "y", -k) for k in range(1, ys)]
    grad_both = sum([grad_both[0].astype(f32)] + [term.astype(f32) for term in got])
    turned_zero = rotate(query_zero, pick(cos_table, 0, 2), pick(sin_table, 0, 2), True).astype(bf16)
    turned_one = rotate(query_one, pick(cos_table, 3, 1), pick(sin_table, 3, 1), True).astype(bf16)
    grad_query = jnp.concatenate(
        [turned_zero[:, :rows], turned_one[:, rows:], turned_zero[:, rows:], turned_one[:, :rows]], axis=1
    )
    grad_qkv = jnp.concatenate(
        [
            grad_query,
            rotate(grad_both[:nk], cos_table, sin_table, True).astype(bf16),
            grad_both[nk:].astype(bf16),
        ],
        axis=0,
    )
    qkv_sent = send_slots([attn_terms(normed_one, grad_qkv, k).astype(bf16) for k in range(1, ys)])
    partial = contract(grad_qkv, qkv_w, 0, 1).astype(bf16)
    mine, beside_sum = scatter_by_c(partial, True)
    beside_sum = beside_sum.astype(bf16)
    from_beside = shift(beside_sum, "x", 1)
    gate_grad = finish(hold(gate_grad, from_beside))
    grad_norm_one = mine + from_beside.astype(f32)
    held = hold(attended, beside_sum)
    output_grad = scatter_whole(
        jnp.concatenate([attn_terms(grad_branch, held, by_y[i]) for i in range(ys)], axis=0).astype(bf16)
    )
    qkv_grad = sum([attn_terms(normed_one, grad_qkv, 0)] + [t.astype(f32) for t in qkv_sent])
    qkv_grad = scatter_column(hold(qkv_grad.astype(bf16), up_grad, beside_sum))
    gain_one_grad = jnp.sum(grad_norm_one * unit_one, axis=0)
    scaled_one = grad_norm_one * gain_one
    up_grad = finish(hold(up_grad, from_beside))
    grad_inputs = grad_middle + scale_one * (
        scaled_one - unit_one * jnp.mean(scaled_one * unit_one, axis=1, keepdims=True)
    )

    qkv_back = finish(qkv_grad)

    def columns(low, high):
        return jnp.concatenate(
            [qkv_back[:, t * nqkv + low : t * nqkv + high] for t in range(4)], axis=1
        ).astype(f32)

    return (
        result,
        from_slots(grad_inputs)[None],
        gain_back(gain_one_grad),
        columns(0, nq),
        columns(nq, nq + nk),
        columns(nq + nk, nqkv),
        finish(output_grad).astype(f32),
        gain_two_back,
        gate_grad.astype(f32),
        up_grad.astype(f32),
        down_grad.astype(f32),
    )


def solution(mesh):
    dp, seq = mesh.shape["dp"], mesh.shape["seq"]
    fine = Mesh(mesh.devices.reshape(dp // 2, 2, seq // 2, 2), ("z", "c", "y", "x"))
    every = ("z", "c", "y", "x")
    tokens = P(("z", "c"), ("y", "x"), None)
    vector, matrix = P(every), P(every, None)
    return jax.shard_map(
        body,
        mesh=fine,
        in_specs=(
            tokens, tokens, P(("z", "c")), P(("z", "c"), None), vector, matrix, matrix, matrix,
            matrix, vector, matrix, matrix, matrix,
        ),
        out_specs=(
            tokens, tokens, vector, matrix, matrix, matrix, matrix, vector, matrix, matrix, matrix,
        ),
        check_vma=False,
    )
```
